32 devices in a mesh: seq: 16 (over z, x, core), head: 2 (over y).
Axes of the slice: x: 2, y: 2, z: 4, core: 2. Of those that a mesh axis runs over, the one named last changes fastest.
Arguments:
- query_input: bfloat16 [14336, 4096], P(('seq', 'head')), may hold values from -12 to 12
- encoded_keys: bfloat16 [14336, 1024], P(('seq', 'head')), may hold values from -8 to 8
- input_values: bfloat16 [14336, 1024], P(('seq', 'head')), may hold values from -6 to 6
- sources: int32 [16, 3], P('seq'), may hold values from -1 to 14, as said below
Outputs:
- attended: bfloat16 [14336, 4096], P(('seq', 'head'))
The draws below stay inside these ranges and needn't reach their ends.
Inputs may be any that keep to these rules, and one draw needn't show every extreme that they name: `sources`: row c: column 0 is c - 1; columns 1 and 2 are c - 2**a and c - 2**b for two different a, b >= 1 with 2**a and 2**b below 16; an entry is -1 where that value is negative.
All inputs are finite; a program needn't handle non-finite values.
Results may differ from the reference program's by a relative error of at most 0.006.
Values may be sent and summed in bfloat16 or wider, within the bound.
A program may use at most 64 MiB of HBM per device.

```python
from functools import reduce
import jax
import jax.numpy as jnp
from jax import lax

QUERY_HEADS = 32
KEY_VALUE_HEADS = 8
HEAD_SIZE = 128
SPAN_TOKENS = 896
SPAN_COUNT = 16
TOKEN_COUNT = 14336


def draw_query_input(key, part):
    key = jax.random.fold_in(key, 3)
    random_noise_key = jax.random.fold_in(key, 0)
    final_result = jnp.clip(2.5 * jax.random.normal(random_noise_key, (TOKEN_COUNT, QUERY_HEADS, HEAD_SIZE), jnp.float32), -10.0, 10.0)
    return final_result.reshape(TOKEN_COUNT, QUERY_HEADS * HEAD_SIZE).astype(jnp.bfloat16)


def draw_encoded_keys(key, part):
    key = jax.random.fold_in(key, 7)
    random_noise_key = jax.random.fold_in(key, 0)
    final_result = jnp.clip(jax.random.normal(random_noise_key, (TOKEN_COUNT, KEY_VALUE_HEADS, HEAD_SIZE), jnp.float32), -5.0, 5.0)
    return final_result.reshape(TOKEN_COUNT, KEY_VALUE_HEADS * HEAD_SIZE).astype(jnp.bfloat16)


def draw_sources(key, part):
    key = jax.random.fold_in(key, 5)
    distances = jnp.array([2 ** power for power in range(1, 31) if 2 ** power < SPAN_COUNT], jnp.int32)
    amount = distances.shape[0]
    first_key, second_key = jax.random.split(key)
    row_index = jnp.arange(SPAN_COUNT, dtype=jnp.int32)
    first_pick = jax.random.randint(first_key, (SPAN_COUNT,), 0, amount)
    forced = SPAN_COUNT - 1 - row_index
    first_pick = jnp.where(forced < amount, forced, first_pick)
    second_pick = (first_pick + jax.random.randint(second_key, (SPAN_COUNT,), 1, amount)) % amount
    table = jnp.stack([row_index - 1, row_index - distances[first_pick], row_index - distances[second_pick]], 1)
    return jnp.where(table >= 0, table, -1).astype(jnp.int32)


def block_levels(rng, dims, cuts, smallest, top_value):
    loudness = 1.0
    for dim, parts in cuts:
        steps = jax.random.uniform(jax.random.fold_in(jax.random.fold_in(rng, 6), dim), (parts,), jnp.float32, smallest / len(cuts), top_value / len(cuts))
        loudness = loudness * jnp.repeat(jnp.exp(steps), dims[dim] // parts).reshape((-1,) + (1,) * (len(dims) - 1 - dim))
    return loudness


def bell_draw(stream_key, dims, scale, limit, pieces=(), kind=jnp.bfloat16):
    loudness = block_levels(stream_key, dims, pieces, -0.22, 0.18) if pieces else 1.0
    entries = jax.random.normal(stream_key, dims, jnp.float32) * scale * loudness
    return jnp.minimum(jnp.maximum(entries, -limit), limit).astype(kind)


def setup_inputs(seed: int = 0) -> dict:
    keys = jax.random.split(jax.random.key(seed), 5)
    query_input = draw_query_input(jax.random.fold_in(keys[4], 71), 0)
    encoded_keys = draw_encoded_keys(jax.random.fold_in(keys[4], 71), 0)
    input_values = bell_draw(keys[2], (TOKEN_COUNT, KEY_VALUE_HEADS * HEAD_SIZE), 1.0, 6.0, ((0, 32),))
    sources = draw_sources(jax.random.fold_in(keys[4], 71), 0)
    return {"query_input": query_input, "encoded_keys": encoded_keys, "input_values": input_values, "sources": sources}


negative_fill = -1e30


def block_terms(query_rows, key_rows, value_rows, causal):
    scores = jnp.einsum("qhd,khd->hqk", query_rows.astype(jnp.float32), key_rows.astype(jnp.float32)) * (HEAD_SIZE ** -0.5)
    if causal:
        position = jnp.arange(query_rows.shape[0])
        allowed = position[:, None] >= position[None, :]
        scores = jnp.where(allowed[None], scores, negative_fill)
    highest = jnp.max(scores, axis=-1)
    weights = jnp.exp(scores - highest[..., None]).astype(jnp.bfloat16)
    row_total = jnp.sum(weights.astype(jnp.float32), axis=-1)
    partial_out = jnp.einsum("hqk,khd->hqd", weights.astype(jnp.float32), value_rows.astype(jnp.float32))
    return highest, row_total, partial_out


def combine(block_list, validity):
    maxima = [jnp.where(is_valid, block_term[0], negative_fill) for block_term, is_valid in zip(block_list, validity)]
    overall = reduce(jnp.maximum, maxima)
    weighted = jnp.zeros(block_list[0][2].shape, jnp.float32)
    normalizer = jnp.zeros(block_list[0][1].shape, jnp.float32)
    for block_term, is_valid in zip(block_list, validity):
        factor = jnp.where(is_valid, jnp.exp(block_term[0] - overall), 0.0)
        weighted = weighted + factor[..., None] * block_term[2]
        normalizer = normalizer + factor * block_term[1]
    return weighted / normalizer[..., None]


def reference(query_input, encoded_keys, input_values, sources):
    group_width = QUERY_HEADS // KEY_VALUE_HEADS
    query_all = query_input.reshape(SPAN_COUNT, SPAN_TOKENS, QUERY_HEADS, HEAD_SIZE)
    keys_combined = encoded_keys.reshape(SPAN_COUNT, SPAN_TOKENS, KEY_VALUE_HEADS, HEAD_SIZE)
    values_combined = input_values.reshape(SPAN_COUNT, SPAN_TOKENS, KEY_VALUE_HEADS, HEAD_SIZE)

    def expand(array_part):
        return jnp.repeat(array_part, group_width, axis=1)

    def one_span(span_index):
        query_rows = query_all[span_index]
        block_list = [block_terms(query_rows, expand(keys_combined[span_index]), expand(values_combined[span_index]), True)]
        validity = [jnp.array(True)]
        for column in range(3):
            source = sources[span_index, column]
            clamped = jnp.maximum(source, 0).astype(jnp.int32)
            block_list.append(block_terms(query_rows, expand(keys_combined[clamped]), expand(values_combined[clamped]), False))
            validity.append(source >= 0)
        final_result = combine(block_list, validity)
        return jnp.transpose(final_result, (1, 0, 2)).reshape(SPAN_TOKENS, QUERY_HEADS * HEAD_SIZE).astype(jnp.bfloat16)

    return lax.map(one_span, jnp.arange(SPAN_COUNT, dtype=jnp.int32)).reshape(TOKEN_COUNT, QUERY_HEADS * HEAD_SIZE)
```

```python
from functools import partial, reduce

import jax
import jax.numpy as jnp
from jax import lax
from jax.experimental import pallas as pl
from jax.experimental.pallas import tpu as pltpu
from jax.sharding import PartitionSpec as P

HEAD_SIZE = 128
LANES = 128
EXPONENT_SCALE = HEAD_SIZE ** (-0.5) * 1.4426950408889634
KEY_HEADS_PER_GROUP = 2

negative_fill = -1e30


def passed_along(value, axis, by):
    devices = lax.axis_size(axis)
    pairs = [(i, i + by) for i in range(devices) if 0 <= i + by < devices]
    return lax.ppermute(value, axis, pairs)


def swapped(value, axis, distance):
    devices = lax.axis_size(axis)
    return lax.ppermute(value, axis, [(i, i ^ distance) for i in range(devices)])


def gather_heads(arrays, offset, widths):
    count = lax.axis_size("head")
    share = [array.shape[1] // count for array in arrays]

    def columns(owner):
        return jnp.concatenate(
            [
                lax.dynamic_slice_in_dim(array, owner * s + offset * w, w, 1)
                for array, s, w in zip(arrays, share, widths)
            ],
            axis=1,
        )

    if count == 2:
        mine = lax.axis_index("head")
        kept = columns(mine)
        arrived = swapped(columns(1 - mine), "head", 1)
        return jnp.where(
            mine == 0,
            jnp.concatenate([kept, arrived], axis=0),
            jnp.concatenate([arrived, kept], axis=0),
        )
    whole = jnp.concatenate([columns(owner) for owner in range(count)], axis=1)
    return lax.all_to_all(whole, "head", split_axis=1, concat_axis=0, tiled=True)


def return_tokens(result):
    count = lax.axis_size("head")
    rows = result.shape[0] // count
    if count == 2:
        mine = lax.axis_index("head")
        kept = lax.dynamic_slice_in_dim(result, mine * rows, rows, 0)
        arrived = swapped(
            lax.dynamic_slice_in_dim(result, (1 - mine) * rows, rows, 0), "head", 1
        )
        return [jnp.where(mine == 0, kept, arrived), jnp.where(mine == 0, arrived, kept)]
    whole = lax.all_to_all(result, "head", split_axis=0, concat_axis=1, tiled=True)
    return jnp.split(whole, count, axis=1)


def attention_kernel(sharing, far_count, choice_ref, query_ref, *refs):
    keys = refs[: 2 + far_count]
    values = refs[2 + far_count : 2 * (2 + far_count)]
    out_ref, key_far, value_all, scores = refs[2 * (2 + far_count) :]
    length = query_ref.shape[0]
    half = length // 2
    near = -(-half // LANES) * LANES

    for block in range(2):
        value_all[block, :, :HEAD_SIZE] = values[block][...]
    value_all[:, :, HEAD_SIZE:] = jnp.ones((4, length, HEAD_SIZE), jnp.bfloat16)
    for column in range(2):
        for number in range(far_count):

            @pl.when(choice_ref[3 + column] == number)
            def _():
                key_far[column] = keys[2 + number][...]
                value_all[2 + column, :, :HEAD_SIZE] = values[2 + number][...]

    valid = [None] + [choice_ref[column] > 0 for column in range(3)]
    scale = [jnp.float32(EXPONENT_SCALE)] + [
        jnp.where(valid[block], EXPONENT_SCALE, 0.0) for block in range(1, 4)
    ]

    def widths(tile):
        return [near if tile == 0 else length, length, length, length]

    def score_block(head, tile, block):
        query = query_ref[
            pl.ds(tile * half, half), pl.ds(pl.multiple_of(head * HEAD_SIZE, HEAD_SIZE), HEAD_SIZE)
        ]
        width = widths(tile)[block]
        key = key_far[block - 2] if block >= 2 else keys[block][:width, :]
        result = lax.dot_general(
            query, key, (((1,), (1,)), ((), ())), preferred_element_type=jnp.float32
        )
        if block == 0:
            row = lax.broadcasted_iota(jnp.int32, result.shape, 0) + tile * half
            column = lax.broadcasted_iota(jnp.int32, result.shape, 1)
            result = jnp.where(column <= row, result, negative_fill)
        scores[tile, block, :, :width] = result
        partial_top = reduce(
            jnp.maximum, [result[:, i : i + LANES] for i in range(0, width, LANES)]
        )
        if block > 0:
            partial_top = jnp.where(valid[block], partial_top, negative_fill)
        return partial_top

    def weigh_block(tile, block, top):
        width = widths(tile)[block]
        shift = top * EXPONENT_SCALE
        if block > 0:
            shift = jnp.where(valid[block], shift, -negative_fill)
        weights = jnp.exp2(scores[tile, block, :, :width] * scale[block] - shift)
        return jnp.dot(
            weights.astype(jnp.bfloat16),
            value_all[block, :width, :],
            preferred_element_type=jnp.float32,
        )

    def top_of(partials):
        return jnp.max(reduce(jnp.maximum, partials), axis=1, keepdims=True)

    def stage(score_head, score_tile, weigh_head, weigh_tile, top):
        partials = []
        total = None
        for block in range(4):
            partials.append(score_block(score_head, score_tile, block))
            part = weigh_block(weigh_tile, block, top)
            total = part if total is None else total + part
        out_ref[
            pl.ds(weigh_tile * half, half),
            pl.ds(pl.multiple_of(weigh_head * HEAD_SIZE, HEAD_SIZE), HEAD_SIZE),
        ] = (total[:, :HEAD_SIZE] / total[:, HEAD_SIZE:]).astype(jnp.bfloat16)
        return top_of(partials)

    first = top_of([score_block(0, 0, block) for block in range(4)])

    def one_head(head, top):
        top = stage(head, 1, head, 0, top)
        return stage(jnp.minimum(head + 1, sharing - 1), 0, head, 1, top)

    lax.fori_loop(0, sharing, one_head, first)


def attention(choice, query, blocks):
    length, width = query.shape
    key_heads = blocks[0].shape[1] // (2 * HEAD_SIZE)
    group = width // key_heads
    query_spec = pl.BlockSpec((length, group), lambda i, *_: (0, i))
    key_spec = pl.BlockSpec((length, HEAD_SIZE), lambda i, *_: (0, i))
    value_spec = pl.BlockSpec((length, HEAD_SIZE), lambda i, *_: (0, i + key_heads))
    flops = 4 * 4 * length * length * width
    return pl.pallas_call(
        partial(attention_kernel, group // HEAD_SIZE, len(blocks) - 2),
        out_shape=jax.ShapeDtypeStruct((length, width), jnp.bfloat16),
        grid_spec=pltpu.PrefetchScalarGridSpec(
            num_scalar_prefetch=1,
            grid=(key_heads,),
            in_specs=[query_spec] + [key_spec] * len(blocks) + [value_spec] * len(blocks),
            out_specs=query_spec,
            scratch_shapes=[
                pltpu.VMEM((2, length, HEAD_SIZE), jnp.bfloat16),
                pltpu.VMEM((4, length, 2 * HEAD_SIZE), jnp.bfloat16),
                pltpu.VMEM((2, 4, length // 2, length), jnp.float32),
            ],
        ),
        cost_estimate=pl.CostEstimate(
            flops=flops, bytes_accessed=4 * length * width, transcendentals=flops // 512
        ),
        compiler_params=pltpu.CompilerParams(vmem_limit_bytes=56 * 1024 * 1024),
    )(choice, query, *blocks, *blocks)


def per_device(query_input, encoded_keys, input_values, sources):
    head_devices = lax.axis_size("head")
    span_count = lax.axis_size("seq")
    own_index = lax.axis_index("seq")
    key_heads = encoded_keys.shape[1] // HEAD_SIZE // head_devices
    sharing = query_input.shape[1] // encoded_keys.shape[1]
    distances = [2**power for power in range(1, 31) if 2**power < span_count]
    row = sources[0]
    distance_table = jnp.array(distances, jnp.int32)
    slots = [
        jnp.sum((distance_table < own_index - row[column]).astype(jnp.int32)) for column in (1, 2)
    ]
    choice = jnp.stack(
        [(row[column] >= 0).astype(jnp.int32) for column in range(3)]
        + [jnp.clip(slot, 0, len(distances) - 1) for slot in slots]
    )
    size = min(KEY_HEADS_PER_GROUP, key_heads)
    width = size * HEAD_SIZE
    pieces = [[] for _ in range(head_devices)]
    for number in range(key_heads // size):
        own = gather_heads([encoded_keys, input_values], number, [width, width])
        query = gather_heads([query_input], number, [width * sharing])
        far = {4: passed_along(own, "seq", 4)}
        far[2] = swapped(jnp.where(own_index // 2 % 2 == 0, own, far[4]), "seq", 2)
        far[1] = swapped(jnp.where(own_index % 2 == 0, own, far[2]), "seq", 1)
        for distance in distances[2:]:
            far[distance] = passed_along(far[distance // 2], "seq", distance // 2)
        result = attention(choice, query, [own, far[1]] + [far[d] for d in distances])
        for owner, piece in enumerate(return_tokens(result)):
            pieces[owner].append(piece)
    return jnp.concatenate([piece for owner in pieces for piece in owner], axis=1)


def solution(mesh):
    in_specs = (
        P(("seq", "head"), None),
        P(("seq", "head"), None),
        P(("seq", "head"), None),
        P("seq", None),
    )
    out_specs = P(("seq", "head"), None)
    return jax.shard_map(
        per_device, mesh=mesh, in_specs=in_specs, out_specs=out_specs, check_vma=False
    )
```

```python
from functools import partial, reduce

import jax
import jax.numpy as jnp
from jax import lax
from jax.experimental import pallas as pl
from jax.experimental.pallas import tpu as pltpu
from jax.sharding import PartitionSpec as P

HEAD_SIZE = 128
LANES = 128
EXPONENT_SCALE = HEAD_SIZE ** (-0.5) * 1.4426950408889634
KEY_HEADS_PER_GROUP = 2

MESH = pl.DeviceIdType.MESH
OWN, ONE, TWO, FOUR, EIGHT = range(5)

negative_fill = -1e30


def passed_along(value, axis, by):
    devices = lax.axis_size(axis)
    pairs = [(i, i + by) for i in range(devices) if 0 <= i + by < devices]
    return lax.ppermute(value, axis, pairs)


def swapped(value, axis, distance):
    devices = lax.axis_size(axis)
    return lax.ppermute(value, axis, [(i, i ^ distance) for i in range(devices)])


def gather_heads(arrays, offset, widths):
    count = lax.axis_size("head")
    share = [array.shape[1] // count for array in arrays]

    def columns(owner):
        return jnp.concatenate(
            [
                lax.dynamic_slice_in_dim(array, owner * s + offset * w, w, 1)
                for array, s, w in zip(arrays, share, widths)
            ],
            axis=1,
        )

    if count == 2:
        mine = lax.axis_index("head")
        kept = columns(mine)
        arrived = swapped(columns(1 - mine), "head", 1)
        return jnp.where(
            mine == 0,
            jnp.concatenate([kept, arrived], axis=0),
            jnp.concatenate([arrived, kept], axis=0),
        )
    whole = jnp.concatenate([columns(owner) for owner in range(count)], axis=1)
    return lax.all_to_all(whole, "head", split_axis=1, concat_axis=0, tiled=True)


def return_tokens(result):
    count = lax.axis_size("head")
    rows = result.shape[0] // count
    if count == 2:
        mine = lax.axis_index("head")
        kept = lax.dynamic_slice_in_dim(result, mine * rows, rows, 0)
        arrived = swapped(
            lax.dynamic_slice_in_dim(result, (1 - mine) * rows, rows, 0), "head", 1
        )
        return [jnp.where(mine == 0, kept, arrived), jnp.where(mine == 0, arrived, kept)]
    whole = lax.all_to_all(result, "head", split_axis=0, concat_axis=1, tiled=True)
    return jnp.split(whole, count, axis=1)


def attention_kernel(sharing, far_count, choice_ref, query_ref, *refs):
    keys = refs[: 2 + far_count]
    values = refs[2 + far_count : 2 * (2 + far_count)]
    out_ref, key_far, value_all, scores = refs[2 * (2 + far_count) :]
    length = query_ref.shape[0]
    half = length // 2
    near = -(-half // LANES) * LANES

    for block in range(2):
        value_all[block, :, :HEAD_SIZE] = values[block][...]
    value_all[:, :, HEAD_SIZE:] = jnp.ones((4, length, HEAD_SIZE), jnp.bfloat16)
    for column in range(2):
        for number in range(far_count):

            @pl.when(choice_ref[3 + column] == number)
            def _():
                key_far[column] = keys[2 + number][...]
                value_all[2 + column, :, :HEAD_SIZE] = values[2 + number][...]

    valid = [None] + [choice_ref[column] > 0 for column in range(3)]
    scale = [jnp.float32(EXPONENT_SCALE)] + [
        jnp.where(valid[block], EXPONENT_SCALE, 0.0) for block in range(1, 4)
    ]

    def widths(tile):
        return [near if tile == 0 else length, length, length, length]

    def score_block(head, tile, block):
        query = query_ref[
            pl.ds(tile * half, half), pl.ds(pl.multiple_of(head * HEAD_SIZE, HEAD_SIZE), HEAD_SIZE)
        ]
        width = widths(tile)[block]
        key = key_far[block - 2] if block >= 2 else keys[block][:width, :]
        result = lax.dot_general(
            query, key, (((1,), (1,)), ((), ())), preferred_element_type=jnp.float32
        )
        if block == 0:
            row = lax.broadcasted_iota(jnp.int32, result.shape, 0) + tile * half
            column = lax.broadcasted_iota(jnp.int32, result.shape, 1)
            result = jnp.where(column <= row, result, negative_fill)
        scores[tile, block, :, :width] = result
        partial_top = reduce(
            jnp.maximum, [result[:, i : i + LANES] for i in range(0, width, LANES)]
        )
        if block > 0:
            partial_top = jnp.where(valid[block], partial_top, negative_fill)
        return partial_top

    def weigh_block(tile, block, top):
        width = widths(tile)[block]
        shift = top * EXPONENT_SCALE
        if block > 0:
            shift = jnp.where(valid[block], shift, -negative_fill)
        weights = jnp.exp2(scores[tile, block, :, :width] * scale[block] - shift)
        return jnp.dot(
            weights.astype(jnp.bfloat16),
            value_all[block, :width, :],
            preferred_element_type=jnp.float32,
        )

    def top_of(partials):
        return jnp.max(reduce(jnp.maximum, partials), axis=1, keepdims=True)

    def stage(score_head, score_tile, weigh_head, weigh_tile, top):
        partials = []
        total = None
        for block in range(4):
            partials.append(score_block(score_head, score_tile, block))
            part = weigh_block(weigh_tile, block, top)
            total = part if total is None else total + part
        out_ref[
            pl.ds(weigh_tile * half, half),
            pl.ds(pl.multiple_of(weigh_head * HEAD_SIZE, HEAD_SIZE), HEAD_SIZE),
        ] = (total[:, :HEAD_SIZE] / total[:, HEAD_SIZE:]).astype(jnp.bfloat16)
        return top_of(partials)

    first = top_of([score_block(0, 0, block) for block in range(4)])

    def one_head(head, top):
        top = stage(head, 1, head, 0, top)
        return stage(jnp.minimum(head + 1, sharing - 1), 0, head, 1, top)

    lax.fori_loop(0, sharing, one_head, first)


def attention(choice, query, blocks):
    length, width = query.shape
    key_heads = blocks[0].shape[1] // (2 * HEAD_SIZE)
    group = width // key_heads
    query_spec = pl.BlockSpec((length, group), lambda i, *_: (0, i))
    key_spec = pl.BlockSpec((length, HEAD_SIZE), lambda i, *_: (0, i))
    value_spec = pl.BlockSpec((length, HEAD_SIZE), lambda i, *_: (0, i + key_heads))
    flops = 4 * 4 * length * length * width
    return pl.pallas_call(
        partial(attention_kernel, group // HEAD_SIZE, len(blocks) - 2),
        out_shape=jax.ShapeDtypeStruct((length, width), jnp.bfloat16),
        grid_spec=pltpu.PrefetchScalarGridSpec(
            num_scalar_prefetch=1,
            grid=(key_heads,),
            in_specs=[query_spec] + [key_spec] * len(blocks) + [value_spec] * len(blocks),
            out_specs=query_spec,
            scratch_shapes=[
                pltpu.VMEM((2, length, HEAD_SIZE), jnp.bfloat16),
                pltpu.VMEM((4, length, 2 * HEAD_SIZE), jnp.bfloat16),
                pltpu.VMEM((2, 4, length // 2, length), jnp.float32),
            ],
        ),
        cost_estimate=pl.CostEstimate(
            flops=flops, bytes_accessed=4 * length * width, transcendentals=flops // 512
        ),
        compiler_params=pltpu.CompilerParams(vmem_limit_bytes=56 * 1024 * 1024),
    )(choice, query, *blocks, *blocks)


def fused_kernel(
    spans, choice_ref, query_ref, key_ref, value_ref, out_ref,
    kv, query_all, result, key_far, value_all, scores,
    local_q, local_kv, send_q, recv_q, send_kv, recv_kv,
    send_four, recv_four, send_chain, recv_chain, local_out, send_out, recv_out,
):
    rows = query_ref.shape[0]
    length = 2 * rows
    groups = kv.shape[1]
    heads = query_all.shape[2] // HEAD_SIZE
    sharing = heads // groups
    near = -(-rows // LANES) * LANES
    span, mine = lax.axis_index("seq"), lax.axis_index("head")
    other = 1 - mine
    odd, odd_pair = span % 2, span // 2 % 2
    beside = span + 1 - 2 * odd
    across = span + 2 - 4 * odd_pair
    has_before, has_after = span >= 4, span < spans - 4

    barrier = pltpu.get_barrier_semaphore()
    for device in ((span, other), (beside, mine), (across, mine)):
        pl.semaphore_signal(barrier, inc=1, device_id=device, device_id_type=MESH)

    @pl.when(has_before)
    def _():
        pl.semaphore_signal(barrier, inc=1, device_id=(span - 4, mine), device_id_type=MESH)

    @pl.when(has_after)
    def _():
        pl.semaphore_signal(barrier, inc=1, device_id=(span + 4, mine), device_id_type=MESH)

    def columns(start, count):
        return pl.ds(pl.multiple_of(start * HEAD_SIZE, HEAD_SIZE), count * HEAD_SIZE)

    def part(index):
        return pl.ds(pl.multiple_of(index * rows, rows), rows)

    def remote(source, target, send, receive, device):
        return pltpu.make_async_remote_copy(
            src_ref=source, dst_ref=target, send_sem=send, recv_sem=receive,
            device_id=device, device_id_type=MESH,
        )

    def kv_local(group, which):
        return pltpu.make_async_copy(
            (key_ref, value_ref)[which].at[:, columns(mine * groups + group, 1)],
            kv.at[OWN, group, which, part(mine), :],
            local_kv.at[group, which],
        )

    def kv_swap(group, which):
        return remote(
            (key_ref, value_ref)[which].at[:, columns(other * groups + group, 1)],
            kv.at[OWN, group, which, part(mine), :],
            send_kv.at[group, which], recv_kv.at[group, which], (span, other),
        )

    def query_local(group):
        return pltpu.make_async_copy(
            query_ref.at[:, columns(mine * heads + group * sharing, sharing)],
            query_all.at[mine, :, columns(group * sharing, sharing)],
            local_q.at[group],
        )

    def query_swap(group):
        return remote(
            query_ref.at[:, columns(other * heads + group * sharing, sharing)],
            query_all.at[mine, :, columns(group * sharing, sharing)],
            send_q.at[group], recv_q.at[group], (span, other),
        )

    def four(group, step):
        rows_part = part(mine) if step == 0 else part(other)
        return remote(
            kv.at[OWN, group, :, rows_part, :], kv.at[FOUR, group, :, rows_part, :],
            send_four.at[group, step], recv_four.at[group, step], (span + 4, mine),
        )

    def chain(group, slot):
        source, device = {
            EIGHT: (FOUR, (span + 4, mine)),
            TWO: (FOUR * odd_pair, (across, mine)),
            ONE: (TWO * odd, (beside, mine)),
        }[slot]
        index = {ONE: 0, TWO: 1, EIGHT: 2}[slot]
        return remote(
            kv.at[source, group], kv.at[slot, group],
            send_chain.at[group, index], recv_chain.at[group, index], device,
        )

    def out_local(head):
        return pltpu.make_async_copy(
            result.at[mine, :, columns(head, 1)],
            out_ref.at[:, columns(mine * heads + head, 1)],
            local_out.at[head],
        )

    def out_swap(head):
        return remote(
            result.at[other, :, columns(head, 1)],
            out_ref.at[:, columns(mine * heads + head, 1)],
            send_out.at[head], recv_out.at[head], (span, other),
        )

    def start_kv(group):
        for which in range(2):
            kv_swap(group, which).start()

    def wait_kv(group):
        for which in range(2):
            kv_swap(group, which).wait_recv()

    def start_four(group, step):
        @pl.when(has_after)
        def _():
            four(group, step).start()

    def wait_four(group):
        @pl.when(has_before)
        def _():
            four(group, 0).wait_recv()
            four(group, 1).wait_recv()

    def start_eight(group):
        @pl.when(jnp.logical_and(has_before, has_after))
        def _():
            chain(group, EIGHT).start()

    def wait_eight(group):
        @pl.when(span >= 8)
        def _():
            chain(group, EIGHT).wait_recv()

    valid = [None] + [choice_ref[column] > 0 for column in range(3)]
    scale = [jnp.float32(EXPONENT_SCALE)] + [
        jnp.where(valid[block], EXPONENT_SCALE, 0.0) for block in range(1, 4)
    ]

    def prepare(group):
        side = group % 2
        for block in range(2):
            value_all[side, block, :, :HEAD_SIZE] = kv[block, group, 1]
        for column in range(2):
            pick = choice_ref[3 + column]
            for which in range(2):
                chosen = lax.select(pick == 1, kv[FOUR, group, which], kv[TWO, group, which])
                chosen = lax.select(pick == 2, kv[EIGHT, group, which], chosen)
                if which == 0:
                    key_far[side, column] = chosen
                else:
                    value_all[side, 2 + column, :, :HEAD_SIZE] = chosen

    def widths(tile):
        return [near if tile == 0 else length, length, length, length]

    def score_block(head, tile, block):
        group = head // sharing
        query = query_all[tile, :, columns(head, 1)]
        width = widths(tile)[block]
        key = key_far[group % 2, block - 2] if block >= 2 else kv[block, group, 0, :width, :]
        scored = lax.dot_general(
            query, key, (((1,), (1,)), ((), ())), preferred_element_type=jnp.float32
        )
        if block == 0:
            row = lax.broadcasted_iota(jnp.int32, scored.shape, 0) + tile * rows
            column = lax.broadcasted_iota(jnp.int32, scored.shape, 1)
            scored = jnp.where(column <= row, scored, negative_fill)
        scores[tile, block, :, :width] = scored
        partial_top = reduce(
            jnp.maximum, [scored[:, i : i + LANES] for i in range(0, width, LANES)]
        )
        if block > 0:
            partial_top = jnp.where(valid[block], partial_top, negative_fill)
        return partial_top

    def weigh_block(head, tile, block, top):
        width = widths(tile)[block]
        shift = top * EXPONENT_SCALE
        if block > 0:
            shift = jnp.where(valid[block], shift, -negative_fill)
        weights = jnp.exp2(scores[tile, block, :, :width] * scale[block] - shift)
        return jnp.dot(
            weights.astype(jnp.bfloat16),
            value_all[head // sharing % 2, block, :width, :],
            preferred_element_type=jnp.float32,
        )

    def top_of(partials):
        return jnp.max(reduce(jnp.maximum, partials), axis=1, keepdims=True)

    def stage(score_head, score_tile, weigh_head, weigh_tile, top):
        partials = []
        total = None
        for block in range(4):
            partials.append(score_block(score_head, score_tile, block))
            term = weigh_block(weigh_head, weigh_tile, block, top)
            total = term if total is None else total + term
        result[weigh_tile, :, columns(weigh_head, 1)] = (
            total[:, :HEAD_SIZE] / total[:, HEAD_SIZE:]
        ).astype(jnp.bfloat16)
        return top_of(partials)

    for group in range(groups):
        for which in range(2):
            kv_local(group, which).start()
    for group in range(groups):
        query_local(group).start()

    pl.semaphore_wait(
        barrier, 3 + jnp.where(has_before, 1, 0) + jnp.where(has_after, 1, 0)
    )
    start_kv(0)
    for side in range(2):
        value_all[side, :, :, HEAD_SIZE:] = jnp.ones((4, length, HEAD_SIZE), jnp.bfloat16)

    @pl.when(jnp.logical_not(has_before))
    def _():
        for group in range(groups):
            kv[FOUR, group] = jnp.zeros(kv.shape[2:], jnp.bfloat16)

    @pl.when(span < 8)
    def _():
        for group in range(groups):
            kv[EIGHT, group] = jnp.zeros(kv.shape[2:], jnp.bfloat16)

    for group in range(groups):
        for which in range(2):
            kv_local(group, which).wait()
    start_four(0, 0)
    wait_kv(0)
    query_swap(0).start()
    start_kv(1)
    start_four(0, 1)

    @pl.when(odd_pair == 0)
    def _():
        chain(0, TWO).start()

    @pl.when(odd == 0)
    def _():
        chain(0, ONE).start()

    wait_four(0)
    start_eight(0)

    @pl.when(odd_pair == 1)
    def _():
        chain(0, TWO).start()

    start_four(1, 0)
    wait_kv(1)
    start_four(1, 1)
    start_kv(2)
    query_swap(1).start()
    chain(0, TWO).wait_recv()

    @pl.when(odd == 1)
    def _():
        chain(0, ONE).start()

    for group in range(groups):
        query_local(group).wait()
    query_swap(0).wait_recv()
    chain(0, ONE).wait_recv()
    wait_eight(0)
    prepare(0)
    first = top_of([score_block(0, 0, block) for block in range(4)])

    def one_head(head, top):
        group = head // sharing
        turn = head % sharing

        @pl.when(jnp.logical_and(turn == 0, group + 2 < groups))
        def _():
            start_four(group + 2, 0)
            wait_kv(group + 2)
            start_four(group + 2, 1)

        @pl.when(jnp.logical_and(turn == 0, group + 1 < groups))
        def _():
            wait_four(group + 1)
            start_eight(group + 1)
            chain(group + 1, TWO).start()

        @pl.when(jnp.logical_and(turn == 2, group + 3 < groups))
        def _():
            start_kv(group + 3)

        @pl.when(jnp.logical_and(turn == 2, group + 2 < groups))
        def _():
            query_swap(group + 2).start()

        @pl.when(jnp.logical_and(turn == 2, group + 1 < groups))
        def _():
            chain(group + 1, TWO).wait_recv()
            chain(group + 1, ONE).start()

        @pl.when(jnp.logical_and(turn == sharing - 1, group + 1 < groups))
        def _():
            query_swap(group + 1).wait_recv()
            chain(group + 1, ONE).wait_recv()
            wait_eight(group + 1)
            prepare(group + 1)

        top = stage(head, 1, head, 0, top)
        top = stage(jnp.minimum(head + 1, heads - 1), 0, head, 1, top)
        out_local(head).start()
        out_swap(head).start()
        return top

    lax.fori_loop(0, heads, one_head, first)

    def settle_group(group, carry):
        for which in range(2):
            kv_swap(group, which).wait_send()
        query_swap(group).wait_send()

        @pl.when(has_after)
        def _():
            four(group, 0).wait_send()
            four(group, 1).wait_send()

        @pl.when(jnp.logical_and(has_before, has_after))
        def _():
            chain(group, EIGHT).wait_send()

        chain(group, TWO).wait_send()
        chain(group, ONE).wait_send()
        return carry

    def settle_head(head, carry):
        out_local(head).wait()
        out_swap(head).wait_send()
        out_swap(head).wait_recv()
        return carry

    lax.fori_loop(0, groups, settle_group, 0)
    lax.fori_loop(0, heads, settle_head, 0)


def fused_attention(choice, query_input, encoded_keys, input_values, spans):
    rows, width = query_input.shape
    groups = encoded_keys.shape[1] // HEAD_SIZE // 2
    heads = width // HEAD_SIZE // 2
    length = 2 * rows
    kept = pl.BlockSpec(memory_space=pl.ANY)
    flops = 4 * 4 * length * length * width // 2
    dma = pltpu.SemaphoreType.DMA
    return pl.pallas_call(
        partial(fused_kernel, spans),
        out_shape=jax.ShapeDtypeStruct((rows, width), jnp.bfloat16),
        in_specs=[pl.BlockSpec(memory_space=pltpu.SMEM), kept, kept, kept],
        out_specs=kept,
        scratch_shapes=[
            pltpu.VMEM((5, groups, 2, length, HEAD_SIZE), jnp.bfloat16),
            pltpu.VMEM((2, rows, heads * HEAD_SIZE), jnp.bfloat16),
            pltpu.VMEM((2, rows, heads * HEAD_SIZE), jnp.bfloat16),
            pltpu.VMEM((2, 2, length, HEAD_SIZE), jnp.bfloat16),
            pltpu.VMEM((2, 4, length, 2 * HEAD_SIZE), jnp.bfloat16),
            pltpu.VMEM((2, 4, rows, length), jnp.float32),
            dma((groups,)), dma((groups, 2)),
            dma((groups,)), dma((groups,)),
            dma((groups, 2)), dma((groups, 2)),
            dma((groups, 2)), dma((groups, 2)),
            dma((groups, 3)), dma((groups, 3)),
            dma((heads,)), dma((heads,)), dma((heads,)),
        ],
        cost_estimate=pl.CostEstimate(
            flops=flops, bytes_accessed=4 * rows * width, transcendentals=flops // 512
        ),
        compiler_params=pltpu.CompilerParams(
            collective_id=0, has_side_effects=True, vmem_limit_bytes=58 * 1024 * 1024
        ),
    )(choice, query_input, encoded_keys, input_values)


def per_device(query_input, encoded_keys, input_values, sources):
    head_devices = lax.axis_size("head")
    span_count = lax.axis_size("seq")
    own_index = lax.axis_index("seq")
    key_heads = encoded_keys.shape[1] // HEAD_SIZE // head_devices
    sharing = query_input.shape[1] // encoded_keys.shape[1]
    distances = [2**power for power in range(1, 31) if 2**power < span_count]
    row = sources[0]
    distance_table = jnp.array(distances, jnp.int32)
    slots = [
        jnp.sum((distance_table < own_index - row[column]).astype(jnp.int32)) for column in (1, 2)
    ]
    choice = jnp.stack(
        [(row[column] >= 0).astype(jnp.int32) for column in range(3)]
        + [jnp.clip(slot, 0, len(distances) - 1) for slot in slots]
    )
    if head_devices == 2 and span_count == 16:
        return fused_attention(choice, query_input, encoded_keys, input_values, span_count)
    size = min(KEY_HEADS_PER_GROUP, key_heads)
    width = size * HEAD_SIZE
    pieces = [[] for _ in range(head_devices)]
    for number in range(key_heads // size):
        own = gather_heads([encoded_keys, input_values], number, [width, width])
        query = gather_heads([query_input], number, [width * sharing])
        far = {4: passed_along(own, "seq", 4)}
        far[2] = swapped(jnp.where(own_index // 2 % 2 == 0, own, far[4]), "seq", 2)
        far[1] = swapped(jnp.where(own_index % 2 == 0, own, far[2]), "seq", 1)
        for distance in distances[2:]:
            far[distance] = passed_along(far[distance // 2], "seq", distance // 2)
        result = attention(choice, query, [own, far[1]] + [far[d] for d in distances])
        for owner, piece in enumerate(return_tokens(result)):
            pieces[owner].append(piece)
    return jnp.concatenate([piece for owner in pieces for piece in owner], axis=1)


def solution(mesh):
    in_specs = (
        P(("seq", "head"), None),
        P(("seq", "head"), None),
        P(("seq", "head"), None),
        P("seq", None),
    )
    out_specs = P(("seq", "head"), None)
    return jax.shard_map(
        per_device, mesh=mesh, in_specs=in_specs, out_specs=out_specs, check_vma=False
    )
```

```python
from functools import partial, reduce

import jax
import jax.numpy as jnp
from jax import lax
from jax.experimental import pallas as pl
from jax.experimental.pallas import tpu as pltpu
from jax.sharding import PartitionSpec as P

HEAD_SIZE = 128
LANES = 128
EXPONENT_SCALE = HEAD_SIZE ** (-0.5) * 1.4426950408889634
KEY_HEADS_PER_GROUP = 2

MESH = pl.DeviceIdType.MESH
OWN, ONE, TWO, FOUR, EIGHT = range(5)

negative_fill = -1e30


def passed_along(value, axis, by):
    devices = lax.axis_size(axis)
    pairs = [(i, i + by) for i in range(devices) if 0 <= i + by < devices]
    return lax.ppermute(value, axis, pairs)


def swapped(value, axis, distance):
    devices = lax.axis_size(axis)
    return lax.ppermute(value, axis, [(i, i ^ distance) for i in range(devices)])


def gather_heads(arrays, offset, widths):
    count = lax.axis_size("head")
    share = [array.shape[1] // count for array in arrays]

    def columns(owner):
        return jnp.concatenate(
            [
                lax.dynamic_slice_in_dim(array, owner * s + offset * w, w, 1)
                for array, s, w in zip(arrays, share, widths)
            ],
            axis=1,
        )

    if count == 2:
        mine = lax.axis_index("head")
        kept = columns(mine)
        arrived = swapped(columns(1 - mine), "head", 1)
        return jnp.where(
            mine == 0,
            jnp.concatenate([kept, arrived], axis=0),
            jnp.concatenate([arrived, kept], axis=0),
        )
    whole = jnp.concatenate([columns(owner) for owner in range(count)], axis=1)
    return lax.all_to_all(whole, "head", split_axis=1, concat_axis=0, tiled=True)


def return_tokens(result):
    count = lax.axis_size("head")
    rows = result.shape[0] // count
    if count == 2:
        mine = lax.axis_index("head")
        kept = lax.dynamic_slice_in_dim(result, mine * rows, rows, 0)
        arrived = swapped(
            lax.dynamic_slice_in_dim(result, (1 - mine) * rows, rows, 0), "head", 1
        )
        return [jnp.where(mine == 0, kept, arrived), jnp.where(mine == 0, arrived, kept)]
    whole = lax.all_to_all(result, "head", split_axis=0, concat_axis=1, tiled=True)
    return jnp.split(whole, count, axis=1)


def attention_kernel(sharing, far_count, choice_ref, query_ref, *refs):
    keys = refs[: 2 + far_count]
    values = refs[2 + far_count : 2 * (2 + far_count)]
    out_ref, key_far, value_all, scores = refs[2 * (2 + far_count) :]
    length = query_ref.shape[0]
    half = length // 2
    near = -(-half // LANES) * LANES

    for block in range(2):
        value_all[block, :, :HEAD_SIZE] = values[block][...]
    value_all[:, :, HEAD_SIZE:] = jnp.ones((4, length, HEAD_SIZE), jnp.bfloat16)
    for column in range(2):
        for number in range(far_count):

            @pl.when(choice_ref[3 + column] == number)
            def _():
                key_far[column] = keys[2 + number][...]
                value_all[2 + column, :, :HEAD_SIZE] = values[2 + number][...]

    valid = [None] + [choice_ref[column] > 0 for column in range(3)]
    scale = [jnp.float32(EXPONENT_SCALE)] + [
        jnp.where(valid[block], EXPONENT_SCALE, 0.0) for block in range(1, 4)
    ]

    def widths(tile):
        return [near if tile == 0 else length, length, length, length]

    def score_block(head, tile, block):
        query = query_ref[
            pl.ds(tile * half, half), pl.ds(pl.multiple_of(head * HEAD_SIZE, HEAD_SIZE), HEAD_SIZE)
        ]
        width = widths(tile)[block]
        key = key_far[block - 2] if block >= 2 else keys[block][:width, :]
        result = lax.dot_general(
            query, key, (((1,), (1,)), ((), ())), preferred_element_type=jnp.float32
        )
        if block == 0:
            row = lax.broadcasted_iota(jnp.int32, result.shape, 0) + tile * half
            column = lax.broadcasted_iota(jnp.int32, result.shape, 1)
            result = jnp.where(column <= row, result, negative_fill)
        scores[tile, block, :, :width] = result
        partial_top = reduce(
            jnp.maximum, [result[:, i : i + LANES] for i in range(0, width, LANES)]
        )
        if block > 0:
            partial_top = jnp.where(valid[block], partial_top, negative_fill)
        return partial_top

    def weigh_block(tile, block, top):
        width = widths(tile)[block]
        shift = top * EXPONENT_SCALE
        if block > 0:
            shift = jnp.where(valid[block], shift, -negative_fill)
        weights = jnp.exp2(scores[tile, block, :, :width] * scale[block] - shift)
        return jnp.dot(
            weights.astype(jnp.bfloat16),
            value_all[block, :width, :],
            preferred_element_type=jnp.float32,
        )

    def top_of(partials):
        return jnp.max(reduce(jnp.maximum, partials), axis=1, keepdims=True)

    def stage(score_head, score_tile, weigh_head, weigh_tile, top):
        partials = []
        total = None
        for block in range(4):
            partials.append(score_block(score_head, score_tile, block))
            part = weigh_block(weigh_tile, block, top)
            total = part if total is None else total + part
        out_ref[
            pl.ds(weigh_tile * half, half),
            pl.ds(pl.multiple_of(weigh_head * HEAD_SIZE, HEAD_SIZE), HEAD_SIZE),
        ] = (total[:, :HEAD_SIZE] / total[:, HEAD_SIZE:]).astype(jnp.bfloat16)
        return top_of(partials)

    first = top_of([score_block(0, 0, block) for block in range(4)])

    def one_head(head, top):
        top = stage(head, 1, head, 0, top)
        return stage(jnp.minimum(head + 1, sharing - 1), 0, head, 1, top)

    lax.fori_loop(0, sharing, one_head, first)


def attention(choice, query, blocks):
    length, width = query.shape
    key_heads = blocks[0].shape[1] // (2 * HEAD_SIZE)
    group = width // key_heads
    query_spec = pl.BlockSpec((length, group), lambda i, *_: (0, i))
    key_spec = pl.BlockSpec((length, HEAD_SIZE), lambda i, *_: (0, i))
    value_spec = pl.BlockSpec((length, HEAD_SIZE), lambda i, *_: (0, i + key_heads))
    flops = 4 * 4 * length * length * width
    return pl.pallas_call(
        partial(attention_kernel, group // HEAD_SIZE, len(blocks) - 2),
        out_shape=jax.ShapeDtypeStruct((length, width), jnp.bfloat16),
        grid_spec=pltpu.PrefetchScalarGridSpec(
            num_scalar_prefetch=1,
            grid=(key_heads,),
            in_specs=[query_spec] + [key_spec] * len(blocks) + [value_spec] * len(blocks),
            out_specs=query_spec,
            scratch_shapes=[
                pltpu.VMEM((2, length, HEAD_SIZE), jnp.bfloat16),
                pltpu.VMEM((4, length, 2 * HEAD_SIZE), jnp.bfloat16),
                pltpu.VMEM((2, 4, length // 2, length), jnp.float32),
            ],
        ),
        cost_estimate=pl.CostEstimate(
            flops=flops, bytes_accessed=4 * length * width, transcendentals=flops // 512
        ),
        compiler_params=pltpu.CompilerParams(vmem_limit_bytes=56 * 1024 * 1024),
    )(choice, query, *blocks, *blocks)


def fused_kernel(
    spans, source_ref, query_ref, key_ref, value_ref, out_ref,
    kv, query_all, result, key_far, value_all, scores,
    local_q, local_kv, send_q, recv_q, send_kv, recv_kv,
    send_four, recv_four, send_chain, recv_chain, local_out, send_out, recv_out,
):
    rows = query_ref.shape[0]
    length = 2 * rows
    groups = kv.shape[1]
    heads = query_all.shape[2] // HEAD_SIZE
    sharing = heads // groups
    near = -(-rows // LANES) * LANES
    span, mine = lax.axis_index("seq"), lax.axis_index("head")
    other = 1 - mine
    odd, odd_pair = span % 2, span // 2 % 2
    beside = span + 1 - 2 * odd
    across = span + 2 - 4 * odd_pair
    has_before, has_after = span >= 4, span < spans - 4

    barrier = pltpu.get_barrier_semaphore()
    for device in ((span, other), (beside, mine), (across, mine)):
        pl.semaphore_signal(barrier, inc=1, device_id=device, device_id_type=MESH)

    @pl.when(has_before)
    def _():
        pl.semaphore_signal(barrier, inc=1, device_id=(span - 4, mine), device_id_type=MESH)

    @pl.when(has_after)
    def _():
        pl.semaphore_signal(barrier, inc=1, device_id=(span + 4, mine), device_id_type=MESH)

    def columns(start, count):
        return pl.ds(pl.multiple_of(start * HEAD_SIZE, HEAD_SIZE), count * HEAD_SIZE)

    def part(index):
        return pl.ds(pl.multiple_of(index * rows, rows), rows)

    def remote(source, target, send, receive, device):
        return pltpu.make_async_remote_copy(
            src_ref=source, dst_ref=target, send_sem=send, recv_sem=receive,
            device_id=device, device_id_type=MESH,
        )

    def kv_local(group, which):
        return pltpu.make_async_copy(
            (key_ref, value_ref)[which].at[:, columns(mine * groups + group, 1)],
            kv.at[OWN, group, which, part(mine), :],
            local_kv.at[group, which],
        )

    def kv_swap(group, which):
        return remote(
            (key_ref, value_ref)[which].at[:, columns(other * groups + group, 1)],
            kv.at[OWN, group, which, part(mine), :],
            send_kv.at[group, which], recv_kv.at[group, which], (span, other),
        )

    def query_local(group):
        return pltpu.make_async_copy(
            query_ref.at[:, columns(mine * heads + group * sharing, sharing)],
            query_all.at[mine, :, columns(group * sharing, sharing)],
            local_q.at[group],
        )

    def query_swap(group):
        return remote(
            query_ref.at[:, columns(other * heads + group * sharing, sharing)],
            query_all.at[mine, :, columns(group * sharing, sharing)],
            send_q.at[group], recv_q.at[group], (span, other),
        )

    def four(group, step):
        rows_part = part(mine) if step == 0 else part(other)
        return remote(
            kv.at[OWN, group, :, rows_part, :], kv.at[FOUR, group, :, rows_part, :],
            send_four.at[group, step], recv_four.at[group, step], (span + 4, mine),
        )

    def chain(group, slot, step):
        source, device = {
            EIGHT: (FOUR, (span + 4, mine)),
            TWO: (FOUR * odd_pair, (across, mine)),
            ONE: (TWO * odd, (beside, mine)),
        }[slot]
        index = {ONE: 0, TWO: 2, EIGHT: 4}[slot] + step
        rows_part = part(mine) if step == 0 else part(other)
        return remote(
            kv.at[source, group, :, rows_part, :], kv.at[slot, group, :, rows_part, :],
            send_chain.at[group, index], recv_chain.at[group, index], device,
        )

    def out_local(head):
        return pltpu.make_async_copy(
            result.at[mine, :, columns(head, 1)],
            out_ref.at[mine, :, columns(head, 1)],
            local_out.at[head],
        )

    def out_swap(head):
        return remote(
            result.at[other, :, columns(head, 1)],
            out_ref.at[mine, :, columns(head, 1)],
            send_out.at[head], recv_out.at[head], (span, other),
        )

    def start_kv(group):
        for which in range(2):
            kv_swap(group, which).start()

    def wait_kv(group):
        for which in range(2):
            kv_swap(group, which).wait_recv()

    def start_four(group, step):
        @pl.when(has_after)
        def _():
            four(group, step).start()

    def wait_four(group, step):
        @pl.when(has_before)
        def _():
            four(group, step).wait_recv()

    def start_eight(group, step):
        @pl.when(jnp.logical_and(has_before, has_after))
        def _():
            chain(group, EIGHT, step).start()

    def wait_eight(group):
        @pl.when(span >= 8)
        def _():
            for step in range(2):
                chain(group, EIGHT, step).wait_recv()

    valid = [None] + [source_ref[0, column] >= 0 for column in range(3)]
    scale = [jnp.float32(EXPONENT_SCALE)] + [
        jnp.where(valid[block], EXPONENT_SCALE, 0.0) for block in range(1, 4)
    ]

    def prepare(group):
        side = group % 2
        for block in range(2):
            value_all[side, block, :, :HEAD_SIZE] = kv[block, group, 1]
        for column in range(2):
            away = span - source_ref[0, 1 + column]
            for which in range(2):
                chosen = lax.select(away == 4, kv[FOUR, group, which], kv[TWO, group, which])
                chosen = lax.select(away == 8, kv[EIGHT, group, which], chosen)
                if which == 0:
                    key_far[side, column] = chosen
                else:
                    value_all[side, 2 + column, :, :HEAD_SIZE] = chosen

    def widths(tile):
        return [near if tile == 0 else length, length, length, length]

    def score_block(head, tile, block):
        group = head // sharing
        query = query_all[tile, :, columns(head, 1)]
        width = widths(tile)[block]
        key = key_far[group % 2, block - 2] if block >= 2 else kv[block, group, 0, :width, :]
        scored = lax.dot_general(
            query, key, (((1,), (1,)), ((), ())), preferred_element_type=jnp.float32
        )
        if block == 0:
            row = lax.broadcasted_iota(jnp.int32, scored.shape, 0) + tile * rows
            column = lax.broadcasted_iota(jnp.int32, scored.shape, 1)
            scored = jnp.where(column <= row, scored, negative_fill)
        scores[tile, block, :, :width] = scored
        partial_top = reduce(
            jnp.maximum, [scored[:, i : i + LANES] for i in range(0, width, LANES)]
        )
        if block > 0:
            partial_top = jnp.where(valid[block], partial_top, negative_fill)
        return partial_top

    def weigh_block(head, tile, block, top):
        width = widths(tile)[block]
        shift = top * EXPONENT_SCALE
        if block > 0:
            shift = jnp.where(valid[block], shift, -negative_fill)
        weights = jnp.exp2(scores[tile, block, :, :width] * scale[block] - shift)
        return jnp.dot(
            weights.astype(jnp.bfloat16),
            value_all[head // sharing % 2, block, :width, :],
            preferred_element_type=jnp.float32,
        )

    def top_of(partials):
        return jnp.max(reduce(jnp.maximum, partials), axis=1, keepdims=True)

    def stage(score_head, score_tile, weigh_head, weigh_tile, top):
        partials = []
        total = None
        for block in range(4):
            partials.append(score_block(score_head, score_tile, block))
            term = weigh_block(weigh_head, weigh_tile, block, top)
            total = term if total is None else total + term
        result[weigh_tile, :, columns(weigh_head, 1)] = (
            total[:, :HEAD_SIZE] / total[:, HEAD_SIZE:]
        ).astype(jnp.bfloat16)
        return top_of(partials)

    for group in range(groups):
        for which in range(2):
            kv_local(group, which).start()
    for group in range(groups):
        query_local(group).start()

    pl.semaphore_wait(
        barrier, 3 + jnp.where(has_before, 1, 0) + jnp.where(has_after, 1, 0)
    )
    start_kv(0)
    for side in range(2):
        value_all[side, :, :, HEAD_SIZE:] = jnp.ones((4, length, HEAD_SIZE), jnp.bfloat16)

    @pl.when(jnp.logical_not(has_before))
    def _():
        for group in range(groups):
            kv[FOUR, group] = jnp.zeros(kv.shape[2:], jnp.bfloat16)

    @pl.when(span < 8)
    def _():
        for group in range(groups):
            kv[EIGHT, group] = jnp.zeros(kv.shape[2:], jnp.bfloat16)

    for which in range(2):
        kv_local(0, which).wait()

    def start_chain(slot, step, bit, value):
        @pl.when(bit == value)
        def _():
            chain(0, slot, step).start()

    start_four(0, 0)
    start_chain(TWO, 0, odd_pair, 0)
    start_chain(ONE, 0, odd, 0)
    wait_kv(0)
    start_four(0, 1)
    start_chain(TWO, 1, odd_pair, 0)
    start_chain(ONE, 1, odd, 0)
    query_swap(0).start()
    for step in range(2):
        wait_four(0, step)
        start_eight(0, step)
        start_chain(TWO, step, odd_pair, 1)
    start_kv(1)
    for step in range(2):
        chain(0, TWO, step).wait_recv()
        start_chain(ONE, step, odd, 1)
    for group in range(1, groups):
        for which in range(2):
            kv_local(group, which).wait()
    for group in range(groups):
        query_local(group).wait()
    query_swap(0).wait_recv()
    query_swap(1).start()
    start_four(1, 0)
    for step in range(2):
        chain(0, ONE, step).wait_recv()
    wait_eight(0)
    wait_kv(1)
    start_four(1, 1)
    prepare(0)
    first = top_of([score_block(0, 0, block) for block in range(4)])

    def one_head(head, top):
        group = head // sharing
        turn = head % sharing

        @pl.when(jnp.logical_and(turn == 0, group + 2 < groups))
        def _():
            start_kv(group + 2)

        @pl.when(jnp.logical_and(turn == 1, group + 2 < groups))
        def _():
            query_swap(group + 2).start()

        @pl.when(jnp.logical_and(turn == 1, group + 1 < groups))
        def _():
            for step in range(2):
                wait_four(group + 1, step)
                start_eight(group + 1, step)
                chain(group + 1, TWO, step).start()

        @pl.when(jnp.logical_and(turn == sharing - 1, group + 2 < groups))
        def _():
            start_four(group + 2, 0)
            wait_kv(group + 2)
            start_four(group + 2, 1)

        @pl.when(jnp.logical_and(turn == sharing - 1, group + 1 < groups))
        def _():
            for step in range(2):
                chain(group + 1, TWO, step).wait_recv()
                chain(group + 1, ONE, step).start()

        top = stage(head, 1, head, 0, top)

        @pl.when(jnp.logical_and(turn == sharing - 1, group + 1 < groups))
        def _():
            query_swap(group + 1).wait_recv()
            for step in range(2):
                chain(group + 1, ONE, step).wait_recv()
            wait_eight(group + 1)
            prepare(group + 1)

        top = stage(jnp.minimum(head + 1, heads - 1), 0, head, 1, top)
        out_local(head).start()
        out_swap(head).start()
        return top

    lax.fori_loop(0, heads, one_head, first)

    def settle_group(group, carry):
        for which in range(2):
            kv_swap(group, which).wait_send()
        query_swap(group).wait_send()

        @pl.when(has_after)
        def _():
            four(group, 0).wait_send()
            four(group, 1).wait_send()

        for step in range(2):
            @pl.when(jnp.logical_and(has_before, has_after))
            def _():
                chain(group, EIGHT, step).wait_send()

            chain(group, TWO, step).wait_send()
            chain(group, ONE, step).wait_send()
        return carry

    def settle_head(head, carry):
        out_local(head).wait()
        out_swap(head).wait_send()
        out_swap(head).wait_recv()
        return carry

    lax.fori_loop(0, groups, settle_group, 0)
    lax.fori_loop(0, heads, settle_head, 0)


def fused_attention(sources, query_input, encoded_keys, input_values, spans):
    rows, width = query_input.shape
    groups = encoded_keys.shape[1] // HEAD_SIZE // 2
    heads = width // HEAD_SIZE // 2
    length = 2 * rows
    kept = pl.BlockSpec(memory_space=pl.ANY)
    flops = 4 * 4 * length * length * width // 2
    dma = pltpu.SemaphoreType.DMA
    halves = pl.pallas_call(
        partial(fused_kernel, spans),
        out_shape=jax.ShapeDtypeStruct((2, rows, width // 2), jnp.bfloat16),
        in_specs=[pl.BlockSpec(memory_space=pltpu.SMEM), kept, kept, kept],
        out_specs=kept,
        scratch_shapes=[
            pltpu.VMEM((5, groups, 2, length, HEAD_SIZE), jnp.bfloat16),
            pltpu.VMEM((2, rows, heads * HEAD_SIZE), jnp.bfloat16),
            pltpu.VMEM((2, rows, heads * HEAD_SIZE), jnp.bfloat16),
            pltpu.VMEM((2, 2, length, HEAD_SIZE), jnp.bfloat16),
            pltpu.VMEM((2, 4, length, 2 * HEAD_SIZE), jnp.bfloat16),
            pltpu.VMEM((2, 4, rows, length), jnp.float32),
            dma((groups,)), dma((groups, 2)),
            dma((groups,)), dma((groups,)),
            dma((groups, 2)), dma((groups, 2)),
            dma((groups, 2)), dma((groups, 2)),
            dma((groups, 6)), dma((groups, 6)),
            dma((heads,)), dma((heads,)), dma((heads,)),
        ],
        cost_estimate=pl.CostEstimate(
            flops=flops, bytes_accessed=4 * rows * width, transcendentals=flops // 512
        ),
        compiler_params=pltpu.CompilerParams(
            collective_id=0, has_side_effects=True, vmem_limit_bytes=58 * 1024 * 1024
        ),
    )(sources, query_input, encoded_keys, input_values)
    return jnp.transpose(halves, (1, 0, 2)).reshape(rows, width)


def per_device(query_input, encoded_keys, input_values, sources):
    head_devices = lax.axis_size("head")
    span_count = lax.axis_size("seq")
    if head_devices == 2 and span_count == 16:
        return fused_attention(sources, query_input, encoded_keys, input_values, span_count)
    own_index = lax.axis_index("seq")
    key_heads = encoded_keys.shape[1] // HEAD_SIZE // head_devices
    sharing = query_input.shape[1] // encoded_keys.shape[1]
    distances = [2**power for power in range(1, 31) if 2**power < span_count]
    row = sources[0]
    distance_table = jnp.array(distances, jnp.int32)
    slots = [
        jnp.sum((distance_table < own_index - row[column]).astype(jnp.int32)) for column in (1, 2)
    ]
    choice = jnp.stack(
        [(row[column] >= 0).astype(jnp.int32) for column in range(3)]
        + [jnp.clip(slot, 0, len(distances) - 1) for slot in slots]
    )
    size = min(KEY_HEADS_PER_GROUP, key_heads)
    width = size * HEAD_SIZE
    pieces = [[] for _ in range(head_devices)]
    for number in range(key_heads // size):
        own = gather_heads([encoded_keys, input_values], number, [width, width])
        query = gather_heads([query_input], number, [width * sharing])
        far = {4: passed_along(own, "seq", 4)}
        far[2] = swapped(jnp.where(own_index // 2 % 2 == 0, own, far[4]), "seq", 2)
        far[1] = swapped(jnp.where(own_index % 2 == 0, own, far[2]), "seq", 1)
        for distance in distances[2:]:
            far[distance] = passed_along(far[distance // 2], "seq", distance // 2)
        result = attention(choice, query, [own, far[1]] + [far[d] for d in distances])
        for owner, piece in enumerate(return_tokens(result)):
            pieces[owner].append(piece)
    return jnp.concatenate([piece for owner in pieces for piece in owner], axis=1)


def solution(mesh):
    in_specs = (
        P(("seq", "head"), None),
        P(("seq", "head"), None),
        P(("seq", "head"), None),
        P("seq", None),
    )
    out_specs = P(("seq", "head"), None)
    return jax.shard_map(
        per_device, mesh=mesh, in_specs=in_specs, out_specs=out_specs, check_vma=False
    )
```

```python
from functools import partial, reduce

import jax
import jax.numpy as jnp
from jax import lax
from jax.experimental import pallas as pl
from jax.experimental.pallas import tpu as pltpu
from jax.sharding import PartitionSpec as P

HEAD_SIZE = 128
LANES = 128
EXPONENT_SCALE = HEAD_SIZE ** (-0.5) * 1.4426950408889634
KEY_HEADS_PER_GROUP = 2

MESH = pl.DeviceIdType.MESH
OWN, ONE, TWO, FOUR, EIGHT = range(5)

negative_fill = -1e30


def passed_along(value, axis, by):
    devices = lax.axis_size(axis)
    pairs = [(i, i + by) for i in range(devices) if 0 <= i + by < devices]
    return lax.ppermute(value, axis, pairs)


def swapped(value, axis, distance):
    devices = lax.axis_size(axis)
    return lax.ppermute(value, axis, [(i, i ^ distance) for i in range(devices)])


def gather_heads(arrays, offset, widths):
    count = lax.axis_size("head")
    share = [array.shape[1] // count for array in arrays]

    def columns(owner):
        return jnp.concatenate(
            [
                lax.dynamic_slice_in_dim(array, owner * s + offset * w, w, 1)
                for array, s, w in zip(arrays, share, widths)
            ],
            axis=1,
        )

    if count == 2:
        mine = lax.axis_index("head")
        kept = columns(mine)
        arrived = swapped(columns(1 - mine), "head", 1)
        return jnp.where(
            mine == 0,
            jnp.concatenate([kept, arrived], axis=0),
            jnp.concatenate([arrived, kept], axis=0),
        )
    whole = jnp.concatenate([columns(owner) for owner in range(count)], axis=1)
    return lax.all_to_all(whole, "head", split_axis=1, concat_axis=0, tiled=True)


def return_tokens(result):
    count = lax.axis_size("head")
    rows = result.shape[0] // count
    if count == 2:
        mine = lax.axis_index("head")
        kept = lax.dynamic_slice_in_dim(result, mine * rows, rows, 0)
        arrived = swapped(
            lax.dynamic_slice_in_dim(result, (1 - mine) * rows, rows, 0), "head", 1
        )
        return [jnp.where(mine == 0, kept, arrived), jnp.where(mine == 0, arrived, kept)]
    whole = lax.all_to_all(result, "head", split_axis=0, concat_axis=1, tiled=True)
    return jnp.split(whole, count, axis=1)


def attention_kernel(sharing, far_count, choice_ref, query_ref, *refs):
    keys = refs[: 2 + far_count]
    values = refs[2 + far_count : 2 * (2 + far_count)]
    out_ref, key_far, value_all, scores = refs[2 * (2 + far_count) :]
    length = query_ref.shape[0]
    half = length // 2
    near = -(-half // LANES) * LANES

    for block in range(2):
        value_all[block, :, :HEAD_SIZE] = values[block][...]
    value_all[:, :, HEAD_SIZE:] = jnp.ones((4, length, HEAD_SIZE), jnp.bfloat16)
    for column in range(2):
        for number in range(far_count):

            @pl.when(choice_ref[3 + column] == number)
            def _():
                key_far[column] = keys[2 + number][...]
                value_all[2 + column, :, :HEAD_SIZE] = values[2 + number][...]

    valid = [None] + [choice_ref[column] > 0 for column in range(3)]
    scale = [jnp.float32(EXPONENT_SCALE)] + [
        jnp.where(valid[block], EXPONENT_SCALE, 0.0) for block in range(1, 4)
    ]

    def widths(tile):
        return [near if tile == 0 else length, length, length, length]

    def score_block(head, tile, block):
        query = query_ref[
            pl.ds(tile * half, half), pl.ds(pl.multiple_of(head * HEAD_SIZE, HEAD_SIZE), HEAD_SIZE)
        ]
        width = widths(tile)[block]
        key = key_far[block - 2] if block >= 2 else keys[block][:width, :]
        result = lax.dot_general(
            query, key, (((1,), (1,)), ((), ())), preferred_element_type=jnp.float32
        )
        if block == 0:
            row = lax.broadcasted_iota(jnp.int32, result.shape, 0) + tile * half
            column = lax.broadcasted_iota(jnp.int32, result.shape, 1)
            result = jnp.where(column <= row, result, negative_fill)
        scores[tile, block, :, :width] = result
        partial_top = reduce(
            jnp.maximum, [result[:, i : i + LANES] for i in range(0, width, LANES)]
        )
        if block > 0:
            partial_top = jnp.where(valid[block], partial_top, negative_fill)
        return partial_top

    def weigh_block(tile, block, top):
        width = widths(tile)[block]
        shift = top * EXPONENT_SCALE
        if block > 0:
            shift = jnp.where(valid[block], shift, -negative_fill)
        weights = jnp.exp2(scores[tile, block, :, :width] * scale[block] - shift)
        return jnp.dot(
            weights.astype(jnp.bfloat16),
            value_all[block, :width, :],
            preferred_element_type=jnp.float32,
        )

    def top_of(partials):
        return jnp.max(reduce(jnp.maximum, partials), axis=1, keepdims=True)

    def stage(score_head, score_tile, weigh_head, weigh_tile, top):
        partials = []
        total = None
        for block in range(4):
            partials.append(score_block(score_head, score_tile, block))
            part = weigh_block(weigh_tile, block, top)
            total = part if total is None else total + part
        out_ref[
            pl.ds(weigh_tile * half, half),
            pl.ds(pl.multiple_of(weigh_head * HEAD_SIZE, HEAD_SIZE), HEAD_SIZE),
        ] = (total[:, :HEAD_SIZE] / total[:, HEAD_SIZE:]).astype(jnp.bfloat16)
        return top_of(partials)

    first = top_of([score_block(0, 0, block) for block in range(4)])

    def one_head(head, top):
        top = stage(head, 1, head, 0, top)
        return stage(jnp.minimum(head + 1, sharing - 1), 0, head, 1, top)

    lax.fori_loop(0, sharing, one_head, first)


def attention(choice, query, blocks):
    length, width = query.shape
    key_heads = blocks[0].shape[1] // (2 * HEAD_SIZE)
    group = width // key_heads
    query_spec = pl.BlockSpec((length, group), lambda i, *_: (0, i))
    key_spec = pl.BlockSpec((length, HEAD_SIZE), lambda i, *_: (0, i))
    value_spec = pl.BlockSpec((length, HEAD_SIZE), lambda i, *_: (0, i + key_heads))
    flops = 4 * 4 * length * length * width
    return pl.pallas_call(
        partial(attention_kernel, group // HEAD_SIZE, len(blocks) - 2),
        out_shape=jax.ShapeDtypeStruct((length, width), jnp.bfloat16),
        grid_spec=pltpu.PrefetchScalarGridSpec(
            num_scalar_prefetch=1,
            grid=(key_heads,),
            in_specs=[query_spec] + [key_spec] * len(blocks) + [value_spec] * len(blocks),
            out_specs=query_spec,
            scratch_shapes=[
                pltpu.VMEM((2, length, HEAD_SIZE), jnp.bfloat16),
                pltpu.VMEM((4, length, 2 * HEAD_SIZE), jnp.bfloat16),
                pltpu.VMEM((2, 4, length // 2, length), jnp.float32),
            ],
        ),
        cost_estimate=pl.CostEstimate(
            flops=flops, bytes_accessed=4 * length * width, transcendentals=flops // 512
        ),
        compiler_params=pltpu.CompilerParams(vmem_limit_bytes=56 * 1024 * 1024),
    )(choice, query, *blocks, *blocks)


def fused_kernel(
    spans, source_ref, query_ref, key_ref, value_ref, out_ref,
    kv, query_all, result, key_far, value_all, scores,
    local_q, local_kv, send_q, recv_q, send_kv, recv_kv,
    send_four, recv_four, send_chain, recv_chain, local_out, send_out, recv_out,
):
    rows = query_ref.shape[0]
    length = 2 * rows
    groups = kv.shape[1]
    heads = query_all.shape[2] // HEAD_SIZE
    sharing = heads // groups
    near = -(-rows // LANES) * LANES
    span, mine = lax.axis_index("seq"), lax.axis_index("head")
    other = 1 - mine
    odd, odd_pair = span % 2, span // 2 % 2
    beside = span + 1 - 2 * odd
    across = span + 2 - 4 * odd_pair
    has_before, has_after = span >= 4, span < spans - 4

    barrier = pltpu.get_barrier_semaphore()
    for device in ((span, other), (beside, mine), (across, mine)):
        pl.semaphore_signal(barrier, inc=1, device_id=device, device_id_type=MESH)

    @pl.when(has_before)
    def _():
        pl.semaphore_signal(barrier, inc=1, device_id=(span - 4, mine), device_id_type=MESH)

    @pl.when(has_after)
    def _():
        pl.semaphore_signal(barrier, inc=1, device_id=(span + 4, mine), device_id_type=MESH)

    def columns(start, count):
        return pl.ds(pl.multiple_of(start * HEAD_SIZE, HEAD_SIZE), count * HEAD_SIZE)

    def part(index):
        return pl.ds(pl.multiple_of(index * rows, rows), rows)

    def remote(source, target, send, receive, device):
        return pltpu.make_async_remote_copy(
            src_ref=source, dst_ref=target, send_sem=send, recv_sem=receive,
            device_id=device, device_id_type=MESH,
        )

    def kv_local(group, which):
        return pltpu.make_async_copy(
            (key_ref, value_ref)[which].at[:, columns(mine * groups + group, 1)],
            kv.at[OWN, group, which, part(mine), :],
            local_kv.at[group, which],
        )

    def kv_swap(group, which):
        return remote(
            (key_ref, value_ref)[which].at[:, columns(other * groups + group, 1)],
            kv.at[OWN, group, which, part(mine), :],
            send_kv.at[group, which], recv_kv.at[group, which], (span, other),
        )

    def query_local(group):
        return pltpu.make_async_copy(
            query_ref.at[:, columns(mine * heads + group * sharing, sharing)],
            query_all.at[mine, :, columns(group * sharing, sharing)],
            local_q.at[group],
        )

    def query_swap(group):
        return remote(
            query_ref.at[:, columns(other * heads + group * sharing, sharing)],
            query_all.at[mine, :, columns(group * sharing, sharing)],
            send_q.at[group], recv_q.at[group], (span, other),
        )

    def four(group, step):
        rows_part = part(mine) if step == 0 else part(other)
        return remote(
            kv.at[OWN, group, :, rows_part, :], kv.at[FOUR, group, :, rows_part, :],
            send_four.at[group, step], recv_four.at[group, step], (span + 4, mine),
        )

    def chain(group, slot, step):
        source, device = {
            EIGHT: (FOUR, (span + 4, mine)),
            TWO: (FOUR * odd_pair, (across, mine)),
            ONE: (TWO * odd, (beside, mine)),
        }[slot]
        index = {ONE: 0, TWO: 2, EIGHT: 4}[slot] + step
        rows_part = part(mine) if step == 0 else part(other)
        return remote(
            kv.at[source, group, :, rows_part, :], kv.at[slot, group, :, rows_part, :],
            send_chain.at[group, index], recv_chain.at[group, index], device,
        )

    def out_local(head):
        return pltpu.make_async_copy(
            result.at[mine, :, columns(head, 1)],
            out_ref.at[mine, :, columns(head, 1)],
            local_out.at[head],
        )

    def out_swap(head):
        return remote(
            result.at[other, :, columns(head, 1)],
            out_ref.at[mine, :, columns(head, 1)],
            send_out.at[head], recv_out.at[head], (span, other),
        )

    def start_kv(group):
        for which in range(2):
            kv_swap(group, which).start()

    def wait_kv(group):
        for which in range(2):
            kv_swap(group, which).wait_recv()

    def start_four(group, step):
        @pl.when(has_after)
        def _():
            four(group, step).start()

    def wait_four(group, step):
        @pl.when(has_before)
        def _():
            four(group, step).wait_recv()

    def start_eight(group, step):
        @pl.when(jnp.logical_and(has_before, has_after))
        def _():
            chain(group, EIGHT, step).start()

    def wait_eight(group):
        @pl.when(span >= 8)
        def _():
            for step in range(2):
                chain(group, EIGHT, step).wait_recv()

    valid = [None] + [source_ref[0, column] >= 0 for column in range(3)]
    scale = [jnp.float32(EXPONENT_SCALE)] + [
        jnp.where(valid[block], EXPONENT_SCALE, 0.0) for block in range(1, 4)
    ]

    def prepare(group):
        side = group % 2
        for block in range(2):
            value_all[side, block, :, :HEAD_SIZE] = kv[block, group, 1]
        for column in range(2):
            away = span - source_ref[0, 1 + column]
            for which in range(2):
                chosen = lax.select(away == 4, kv[FOUR, group, which], kv[TWO, group, which])
                chosen = lax.select(away == 8, kv[EIGHT, group, which], chosen)
                if which == 0:
                    key_far[side, column] = chosen
                else:
                    value_all[side, 2 + column, :, :HEAD_SIZE] = chosen

    def widths(tile):
        return [near if tile == 0 else length, length, length, length]

    def score_block(head, tile, block):
        group = head // sharing
        query = query_all[tile, :, columns(head, 1)]
        width = widths(tile)[block]
        key = key_far[group % 2, block - 2] if block >= 2 else kv[block, group, 0, :width, :]
        scored = lax.dot_general(
            query, key, (((1,), (1,)), ((), ())), preferred_element_type=jnp.float32
        )
        if block == 0:
            row = lax.broadcasted_iota(jnp.int32, scored.shape, 0) + tile * rows
            column = lax.broadcasted_iota(jnp.int32, scored.shape, 1)
            scored = jnp.where(column <= row, scored, negative_fill)
        scores[tile, block, :, :width] = scored
        partial_top = reduce(
            jnp.maximum, [scored[:, i : i + LANES] for i in range(0, width, LANES)]
        )
        if block > 0:
            partial_top = jnp.where(valid[block], partial_top, negative_fill)
        return partial_top

    def weigh_block(head, tile, block, top):
        width = widths(tile)[block]
        shift = top * EXPONENT_SCALE
        if block > 0:
            shift = jnp.where(valid[block], shift, -negative_fill)
        weights = jnp.exp2(scores[tile, block, :, :width] * scale[block] - shift)
        return jnp.dot(
            weights.astype(jnp.bfloat16),
            value_all[head // sharing % 2, block, :width, :],
            preferred_element_type=jnp.float32,
        )

    def top_of(partials):
        return jnp.max(reduce(jnp.maximum, partials), axis=1, keepdims=True)

    def store(head, tile, total):
        result[tile, :, columns(head, 1)] = (
            total[:, :HEAD_SIZE] / total[:, HEAD_SIZE:]
        ).astype(jnp.bfloat16)

    def stage(score_head, score_tile, weigh_head, weigh_tile, top):
        partials = []
        total = None
        for block in range(4):
            partials.append(score_block(score_head, score_tile, block))
            term = weigh_block(weigh_head, weigh_tile, block, top)
            total = term if total is None else total + term
        store(weigh_head, weigh_tile, total)
        return top_of(partials)

    for group in range(groups):
        for which in range(2):
            kv_local(group, which).start()
    for group in range(groups):
        query_local(group).start()

    pl.semaphore_wait(
        barrier, 3 + jnp.where(has_before, 1, 0) + jnp.where(has_after, 1, 0)
    )
    start_kv(0)
    for side in range(2):
        value_all[side, :, :, HEAD_SIZE:] = jnp.ones((4, length, HEAD_SIZE), jnp.bfloat16)

    @pl.when(jnp.logical_not(has_before))
    def _():
        for group in range(groups):
            kv[FOUR, group] = jnp.zeros(kv.shape[2:], jnp.bfloat16)

    @pl.when(span < 8)
    def _():
        for group in range(groups):
            kv[EIGHT, group] = jnp.zeros(kv.shape[2:], jnp.bfloat16)

    for which in range(2):
        kv_local(0, which).wait()

    def start_chain(slot, step, bit, value):
        @pl.when(bit == value)
        def _():
            chain(0, slot, step).start()

    start_four(0, 0)
    start_chain(TWO, 0, odd_pair, 0)
    start_chain(ONE, 0, odd, 0)
    wait_kv(0)
    start_four(0, 1)
    start_chain(TWO, 1, odd_pair, 0)
    start_chain(ONE, 1, odd, 0)
    query_swap(0).start()
    for step in range(2):
        wait_four(0, step)
        start_eight(0, step)
        start_chain(TWO, step, odd_pair, 1)
    start_kv(1)
    for step in range(2):
        chain(0, TWO, step).wait_recv()
        start_chain(ONE, step, odd, 1)
    for group in range(1, groups):
        for which in range(2):
            kv_local(group, which).wait()
    for group in range(groups):
        query_local(group).wait()
    query_swap(0).wait_recv()
    query_swap(1).start()
    start_four(1, 0)
    for step in range(2):
        chain(0, ONE, step).wait_recv()
    wait_eight(0)
    wait_kv(1)
    start_four(1, 1)
    prepare(0)
    start_kv(2)
    first = top_of([score_block(0, 0, block) for block in range(4)])
    first = stage(0, 1, 0, 0, first)

    def one_head(head, top):
        group = head // sharing
        turn = head % sharing

        @pl.when(turn == 0)
        def _():
            query_swap(group).wait_recv()
            for step in range(2):
                chain(group, ONE, step).wait_recv()
            wait_eight(group)
            prepare(group)

        @pl.when(jnp.logical_and(turn == 0, group + 2 < groups))
        def _():
            start_kv(group + 2)

        @pl.when(jnp.logical_and(turn == 1, group + 2 < groups))
        def _():
            query_swap(group + 2).start()

        @pl.when(jnp.logical_and(turn == 1, group + 1 < groups))
        def _():
            for step in range(2):
                wait_four(group + 1, step)
                start_eight(group + 1, step)
                chain(group + 1, TWO, step).start()

        @pl.when(jnp.logical_and(turn == sharing - 2, group + 2 < groups))
        def _():
            start_four(group + 2, 0)
            wait_kv(group + 2)
            start_four(group + 2, 1)

        @pl.when(jnp.logical_and(turn == sharing - 1, group + 1 < groups))
        def _():
            for step in range(2):
                chain(group + 1, TWO, step).wait_recv()
                chain(group + 1, ONE, step).start()

        top = stage(head, 0, head - 1, 1, top)
        top = stage(head, 1, head, 0, top)
        out_local(head - 1).start()
        out_swap(head - 1).start()
        return top

    last = lax.fori_loop(1, heads, one_head, first)
    store(
        heads - 1, 1, reduce(jnp.add, [weigh_block(heads - 1, 1, block, last) for block in range(4)])
    )
    out_local(heads - 1).start()
    out_swap(heads - 1).start()

    def settle_group(group, carry):
        for which in range(2):
            kv_swap(group, which).wait_send()
        query_swap(group).wait_send()

        @pl.when(has_after)
        def _():
            four(group, 0).wait_send()
            four(group, 1).wait_send()

        for step in range(2):
            @pl.when(jnp.logical_and(has_before, has_after))
            def _():
                chain(group, EIGHT, step).wait_send()

            chain(group, TWO, step).wait_send()
            chain(group, ONE, step).wait_send()
        return carry

    def settle_head(head, carry):
        out_local(head).wait()
        out_swap(head).wait_send()
        out_swap(head).wait_recv()
        return carry

    lax.fori_loop(0, groups, settle_group, 0)
    lax.fori_loop(0, heads, settle_head, 0)


def fused_attention(sources, query_input, encoded_keys, input_values, spans):
    rows, width = query_input.shape
    groups = encoded_keys.shape[1] // HEAD_SIZE // 2
    heads = width // HEAD_SIZE // 2
    length = 2 * rows
    kept = pl.BlockSpec(memory_space=pl.ANY)
    flops = 4 * 4 * length * length * width // 2
    dma = pltpu.SemaphoreType.DMA
    halves = pl.pallas_call(
        partial(fused_kernel, spans),
        out_shape=jax.ShapeDtypeStruct((2, rows, width // 2), jnp.bfloat16),
        in_specs=[pl.BlockSpec(memory_space=pltpu.SMEM), kept, kept, kept],
        out_specs=kept,
        scratch_shapes=[
            pltpu.VMEM((5, groups, 2, length, HEAD_SIZE), jnp.bfloat16),
            pltpu.VMEM((2, rows, heads * HEAD_SIZE), jnp.bfloat16),
            pltpu.VMEM((2, rows, heads * HEAD_SIZE), jnp.bfloat16),
            pltpu.VMEM((2, 2, length, HEAD_SIZE), jnp.bfloat16),
            pltpu.VMEM((2, 4, length, 2 * HEAD_SIZE), jnp.bfloat16),
            pltpu.VMEM((2, 4, rows, length), jnp.float32),
            dma((groups,)), dma((groups, 2)),
            dma((groups,)), dma((groups,)),
            dma((groups, 2)), dma((groups, 2)),
            dma((groups, 2)), dma((groups, 2)),
            dma((groups, 6)), dma((groups, 6)),
            dma((heads,)), dma((heads,)), dma((heads,)),
        ],
        cost_estimate=pl.CostEstimate(
            flops=flops, bytes_accessed=4 * rows * width, transcendentals=flops // 512
        ),
        compiler_params=pltpu.CompilerParams(
            collective_id=0, has_side_effects=True, vmem_limit_bytes=58 * 1024 * 1024
        ),
    )(sources, query_input, encoded_keys, input_values)
    return jnp.transpose(halves, (1, 0, 2)).reshape(rows, width)


def per_device(query_input, encoded_keys, input_values, sources):
    head_devices = lax.axis_size("head")
    span_count = lax.axis_size("seq")
    if head_devices == 2 and span_count == 16:
        return fused_attention(sources, query_input, encoded_keys, input_values, span_count)
    own_index = lax.axis_index("seq")
    key_heads = encoded_keys.shape[1] // HEAD_SIZE // head_devices
    sharing = query_input.shape[1] // encoded_keys.shape[1]
    distances = [2**power for power in range(1, 31) if 2**power < span_count]
    row = sources[0]
    distance_table = jnp.array(distances, jnp.int32)
    slots = [
        jnp.sum((distance_table < own_index - row[column]).astype(jnp.int32)) for column in (1, 2)
    ]
    choice = jnp.stack(
        [(row[column] >= 0).astype(jnp.int32) for column in range(3)]
        + [jnp.clip(slot, 0, len(distances) - 1) for slot in slots]
    )
    size = min(KEY_HEADS_PER_GROUP, key_heads)
    width = size * HEAD_SIZE
    pieces = [[] for _ in range(head_devices)]
    for number in range(key_heads // size):
        own = gather_heads([encoded_keys, input_values], number, [width, width])
        query = gather_heads([query_input], number, [width * sharing])
        far = {4: passed_along(own, "seq", 4)}
        far[2] = swapped(jnp.where(own_index // 2 % 2 == 0, own, far[4]), "seq", 2)
        far[1] = swapped(jnp.where(own_index % 2 == 0, own, far[2]), "seq", 1)
        for distance in distances[2:]:
            far[distance] = passed_along(far[distance // 2], "seq", distance // 2)
        result = attention(choice, query, [own, far[1]] + [far[d] for d in distances])
        for owner, piece in enumerate(return_tokens(result)):
            pieces[owner].append(piece)
    return jnp.concatenate([piece for owner in pieces for piece in owner], axis=1)


def solution(mesh):
    in_specs = (
        P(("seq", "head"), None),
        P(("seq", "head"), None),
        P(("seq", "head"), None),
        P("seq", None),
    )
    out_specs = P(("seq", "head"), None)
    return jax.shard_map(
        per_device, mesh=mesh, in_specs=in_specs, out_specs=out_specs, check_vma=False
    )
```

```python
from functools import partial, reduce

import jax
import jax.numpy as jnp
from jax import lax
from jax.experimental import pallas as pl
from jax.experimental.pallas import tpu as pltpu
from jax.sharding import PartitionSpec as P

HEAD_SIZE = 128
LANES = 128
EXPONENT_SCALE = HEAD_SIZE ** (-0.5) * 1.4426950408889634
KEY_HEADS_PER_GROUP = 2

MESH = pl.DeviceIdType.MESH
OWN, ONE, TWO, FOUR, EIGHT = range(5)

negative_fill = -1e30


def passed_along(value, axis, by):
    devices = lax.axis_size(axis)
    pairs = [(i, i + by) for i in range(devices) if 0 <= i + by < devices]
    return lax.ppermute(value, axis, pairs)


def swapped(value, axis, distance):
    devices = lax.axis_size(axis)
    return lax.ppermute(value, axis, [(i, i ^ distance) for i in range(devices)])


def gather_heads(arrays, offset, widths):
    count = lax.axis_size("head")
    share = [array.shape[1] // count for array in arrays]

    def columns(owner):
        return jnp.concatenate(
            [
                lax.dynamic_slice_in_dim(array, owner * s + offset * w, w, 1)
                for array, s, w in zip(arrays, share, widths)
            ],
            axis=1,
        )

    if count == 2:
        mine = lax.axis_index("head")
        kept = columns(mine)
        arrived = swapped(columns(1 - mine), "head", 1)
        return jnp.where(
            mine == 0,
            jnp.concatenate([kept, arrived], axis=0),
            jnp.concatenate([arrived, kept], axis=0),
        )
    whole = jnp.concatenate([columns(owner) for owner in range(count)], axis=1)
    return lax.all_to_all(whole, "head", split_axis=1, concat_axis=0, tiled=True)


def return_tokens(result):
    count = lax.axis_size("head")
    rows = result.shape[0] // count
    if count == 2:
        mine = lax.axis_index("head")
        kept = lax.dynamic_slice_in_dim(result, mine * rows, rows, 0)
        arrived = swapped(
            lax.dynamic_slice_in_dim(result, (1 - mine) * rows, rows, 0), "head", 1
        )
        return [jnp.where(mine == 0, kept, arrived), jnp.where(mine == 0, arrived, kept)]
    whole = lax.all_to_all(result, "head", split_axis=0, concat_axis=1, tiled=True)
    return jnp.split(whole, count, axis=1)


def attention_kernel(sharing, far_count, choice_ref, query_ref, *refs):
    keys = refs[: 2 + far_count]
    values = refs[2 + far_count : 2 * (2 + far_count)]
    out_ref, key_far, value_all, scores = refs[2 * (2 + far_count) :]
    length = query_ref.shape[0]
    half = length // 2
    near = -(-half // LANES) * LANES

    for block in range(2):
        value_all[block, :, :HEAD_SIZE] = values[block][...]
    value_all[:, :, HEAD_SIZE:] = jnp.ones((4, length, HEAD_SIZE), jnp.bfloat16)
    for column in range(2):
        for number in range(far_count):

            @pl.when(choice_ref[3 + column] == number)
            def _():
                key_far[column] = keys[2 + number][...]
                value_all[2 + column, :, :HEAD_SIZE] = values[2 + number][...]

    valid = [None] + [choice_ref[column] > 0 for column in range(3)]
    scale = [jnp.float32(EXPONENT_SCALE)] + [
        jnp.where(valid[block], EXPONENT_SCALE, 0.0) for block in range(1, 4)
    ]

    def widths(tile):
        return [near if tile == 0 else length, length, length, length]

    def score_block(head, tile, block):
        query = query_ref[
            pl.ds(tile * half, half), pl.ds(pl.multiple_of(head * HEAD_SIZE, HEAD_SIZE), HEAD_SIZE)
        ]
        width = widths(tile)[block]
        key = key_far[block - 2] if block >= 2 else keys[block][:width, :]
        result = lax.dot_general(
            query, key, (((1,), (1,)), ((), ())), preferred_element_type=jnp.float32
        )
        if block == 0:
            row = lax.broadcasted_iota(jnp.int32, result.shape, 0) + tile * half
            column = lax.broadcasted_iota(jnp.int32, result.shape, 1)
            result = jnp.where(column <= row, result, negative_fill)
        scores[tile, block, :, :width] = result
        partial_top = reduce(
            jnp.maximum, [result[:, i : i + LANES] for i in range(0, width, LANES)]
        )
        if block > 0:
            partial_top = jnp.where(valid[block], partial_top, negative_fill)
        return partial_top

    def weigh_block(tile, block, top):
        width = widths(tile)[block]
        shift = top * EXPONENT_SCALE
        if block > 0:
            shift = jnp.where(valid[block], shift, -negative_fill)
        weights = jnp.exp2(scores[tile, block, :, :width] * scale[block] - shift)
        return jnp.dot(
            weights.astype(jnp.bfloat16),
            value_all[block, :width, :],
            preferred_element_type=jnp.float32,
        )

    def top_of(partials):
        return jnp.max(reduce(jnp.maximum, partials), axis=1, keepdims=True)

    def stage(score_head, score_tile, weigh_head, weigh_tile, top):
        partials = []
        total = None
        for block in range(4):
            partials.append(score_block(score_head, score_tile, block))
            part = weigh_block(weigh_tile, block, top)
            total = part if total is None else total + part
        out_ref[
            pl.ds(weigh_tile * half, half),
            pl.ds(pl.multiple_of(weigh_head * HEAD_SIZE, HEAD_SIZE), HEAD_SIZE),
        ] = (total[:, :HEAD_SIZE] / total[:, HEAD_SIZE:]).astype(jnp.bfloat16)
        return top_of(partials)

    first = top_of([score_block(0, 0, block) for block in range(4)])

    def one_head(head, top):
        top = stage(head, 1, head, 0, top)
        return stage(jnp.minimum(head + 1, sharing - 1), 0, head, 1, top)

    lax.fori_loop(0, sharing, one_head, first)


def attention(choice, query, blocks):
    length, width = query.shape
    key_heads = blocks[0].shape[1] // (2 * HEAD_SIZE)
    group = width // key_heads
    query_spec = pl.BlockSpec((length, group), lambda i, *_: (0, i))
    key_spec = pl.BlockSpec((length, HEAD_SIZE), lambda i, *_: (0, i))
    value_spec = pl.BlockSpec((length, HEAD_SIZE), lambda i, *_: (0, i + key_heads))
    flops = 4 * 4 * length * length * width
    return pl.pallas_call(
        partial(attention_kernel, group // HEAD_SIZE, len(blocks) - 2),
        out_shape=jax.ShapeDtypeStruct((length, width), jnp.bfloat16),
        grid_spec=pltpu.PrefetchScalarGridSpec(
            num_scalar_prefetch=1,
            grid=(key_heads,),
            in_specs=[query_spec] + [key_spec] * len(blocks) + [value_spec] * len(blocks),
            out_specs=query_spec,
            scratch_shapes=[
                pltpu.VMEM((2, length, HEAD_SIZE), jnp.bfloat16),
                pltpu.VMEM((4, length, 2 * HEAD_SIZE), jnp.bfloat16),
                pltpu.VMEM((2, 4, length // 2, length), jnp.float32),
            ],
        ),
        cost_estimate=pl.CostEstimate(
            flops=flops, bytes_accessed=4 * length * width, transcendentals=flops // 512
        ),
        compiler_params=pltpu.CompilerParams(vmem_limit_bytes=56 * 1024 * 1024),
    )(choice, query, *blocks, *blocks)


def fused_kernel(
    spans, source_ref, query_ref, key_ref, value_ref, out_ref,
    kv, query_all, result, key_far, value_all, scores,
    local_q, local_kv, send_q, recv_q, send_kv, recv_kv,
    send_four, recv_four, send_chain, recv_chain, local_out, send_out, recv_out,
):
    rows = query_ref.shape[0]
    length = 2 * rows
    groups = kv.shape[1]
    heads = query_all.shape[2] // HEAD_SIZE
    sharing = heads // groups
    near = -(-rows // LANES) * LANES
    span, mine = lax.axis_index("seq"), lax.axis_index("head")
    other = 1 - mine
    odd, odd_pair = span % 2, span // 2 % 2
    beside = span + 1 - 2 * odd
    across = span + 2 - 4 * odd_pair
    has_before, has_after = span >= 4, span < spans - 4

    barrier = pltpu.get_barrier_semaphore()
    for device in ((span, other), (beside, mine), (across, mine)):
        pl.semaphore_signal(barrier, inc=1, device_id=device, device_id_type=MESH)

    @pl.when(has_before)
    def _():
        pl.semaphore_signal(barrier, inc=1, device_id=(span - 4, mine), device_id_type=MESH)

    @pl.when(has_after)
    def _():
        pl.semaphore_signal(barrier, inc=1, device_id=(span + 4, mine), device_id_type=MESH)

    def columns(start, count):
        return pl.ds(pl.multiple_of(start * HEAD_SIZE, HEAD_SIZE), count * HEAD_SIZE)

    def part(index):
        return pl.ds(pl.multiple_of(index * rows, rows), rows)

    def remote(source, target, send, receive, device):
        return pltpu.make_async_remote_copy(
            src_ref=source, dst_ref=target, send_sem=send, recv_sem=receive,
            device_id=device, device_id_type=MESH,
        )

    def kv_local(group, which):
        return pltpu.make_async_copy(
            (key_ref, value_ref)[which].at[:, columns(mine * groups + group, 1)],
            kv.at[OWN, group, which, part(mine), :],
            local_kv.at[group, which],
        )

    def kv_swap(group, which):
        return remote(
            (key_ref, value_ref)[which].at[:, columns(other * groups + group, 1)],
            kv.at[OWN, group, which, part(mine), :],
            send_kv.at[group, which], recv_kv.at[group, which], (span, other),
        )

    def query_local(group):
        return pltpu.make_async_copy(
            query_ref.at[:, columns(mine * heads + group * sharing, sharing)],
            query_all.at[mine, :, columns(group * sharing, sharing)],
            local_q.at[group],
        )

    def query_swap(group):
        return remote(
            query_ref.at[:, columns(other * heads + group * sharing, sharing)],
            query_all.at[mine, :, columns(group * sharing, sharing)],
            send_q.at[group], recv_q.at[group], (span, other),
        )

    def four(group, step):
        rows_part = part(mine) if step == 0 else part(other)
        return remote(
            kv.at[OWN, group, :, rows_part, :], kv.at[FOUR, group, :, rows_part, :],
            send_four.at[group, step], recv_four.at[group, step], (span + 4, mine),
        )

    def chain(group, slot, step):
        source, device = {
            EIGHT: (FOUR, (span + 4, mine)),
            TWO: (FOUR * odd_pair, (across, mine)),
            ONE: (TWO * odd, (beside, mine)),
        }[slot]
        index = {ONE: 0, TWO: 2, EIGHT: 4}[slot] + step
        rows_part = part(mine) if step == 0 else part(other)
        return remote(
            kv.at[source, group, :, rows_part, :], kv.at[slot, group, :, rows_part, :],
            send_chain.at[group, index], recv_chain.at[group, index], device,
        )

    def out_local(head):
        return pltpu.make_async_copy(
            result.at[mine, :, columns(head, 1)],
            out_ref.at[mine, :, columns(head, 1)],
            local_out.at[head],
        )

    def out_swap(head):
        return remote(
            result.at[other, :, columns(head, 1)],
            out_ref.at[mine, :, columns(head, 1)],
            send_out.at[head], recv_out.at[head], (span, other),
        )

    def start_kv(group):
        for which in range(2):
            kv_swap(group, which).start()

    def wait_kv(group):
        for which in range(2):
            kv_swap(group, which).wait_recv()

    def start_four(group, step):
        @pl.when(has_after)
        def _():
            four(group, step).start()

    def wait_four(group, step):
        @pl.when(has_before)
        def _():
            four(group, step).wait_recv()

    def start_eight(group, step):
        @pl.when(jnp.logical_and(has_before, has_after))
        def _():
            chain(group, EIGHT, step).start()

    def wait_eight(group):
        @pl.when(span >= 8)
        def _():
            for step in range(2):
                chain(group, EIGHT, step).wait_recv()

    valid = [None] + [source_ref[0, column] >= 0 for column in range(3)]
    scale = [jnp.float32(EXPONENT_SCALE)] + [
        jnp.where(valid[block], EXPONENT_SCALE, 0.0) for block in range(1, 4)
    ]

    def prepare(group):
        side = group % 2
        for block in range(2):
            value_all[side, block, :, :HEAD_SIZE] = kv[block, group, 1]
        for column in range(2):
            away = span - source_ref[0, 1 + column]
            for which in range(2):
                chosen = lax.select(away == 4, kv[FOUR, group, which], kv[TWO, group, which])
                chosen = lax.select(away == 8, kv[EIGHT, group, which], chosen)
                if which == 0:
                    key_far[side, column] = chosen
                else:
                    value_all[side, 2 + column, :, :HEAD_SIZE] = chosen

    def widths(tile):
        return [near if tile == 0 else length, length, length, length]

    def score_block(head, tile, block):
        group = head // sharing
        query = query_all[tile, :, columns(head, 1)]
        width = widths(tile)[block]
        key = key_far[group % 2, block - 2] if block >= 2 else kv[block, group, 0, :width, :]
        scored = lax.dot_general(
            query, key, (((1,), (1,)), ((), ())), preferred_element_type=jnp.float32
        )
        if block == 0:
            start = tile * rows // LANES * LANES
            edge = scored[:, start:]
            row = lax.broadcasted_iota(jnp.int32, edge.shape, 0) + tile * rows
            column = lax.broadcasted_iota(jnp.int32, edge.shape, 1) + start
            edge = jnp.where(column <= row, edge, negative_fill)
            scored = jnp.concatenate([scored[:, :start], edge], axis=1) if start else edge
        scores[tile, block, :, :width] = scored
        partial_top = reduce(
            jnp.maximum, [scored[:, i : i + LANES] for i in range(0, width, LANES)]
        )
        if block > 0:
            partial_top = jnp.where(valid[block], partial_top, negative_fill)
        return partial_top

    def weigh_block(head, tile, block, top):
        width = widths(tile)[block]
        shift = top * EXPONENT_SCALE
        if block > 0:
            shift = jnp.where(valid[block], shift, -negative_fill)
        weights = jnp.exp2(scores[tile, block, :, :width] * scale[block] - shift)
        return jnp.dot(
            weights.astype(jnp.bfloat16),
            value_all[head // sharing % 2, block, :width, :],
            preferred_element_type=jnp.float32,
        )

    def top_of(partials):
        return jnp.max(reduce(jnp.maximum, partials), axis=1, keepdims=True)

    def store(head, tile, total):
        result[tile, :, columns(head, 1)] = (
            total[:, :HEAD_SIZE] / total[:, HEAD_SIZE:]
        ).astype(jnp.bfloat16)

    def stage(score_head, score_tile, weigh_head, weigh_tile, top):
        partials = []
        total = None
        for block in range(4):
            partials.append(score_block(score_head, score_tile, block))
            term = weigh_block(weigh_head, weigh_tile, block, top)
            total = term if total is None else total + term
        store(weigh_head, weigh_tile, total)
        return top_of(partials)

    for group in range(groups):
        for which in range(2):
            kv_local(group, which).start()
    for group in range(groups):
        query_local(group).start()

    pl.semaphore_wait(
        barrier, 3 + jnp.where(has_before, 1, 0) + jnp.where(has_after, 1, 0)
    )
    start_kv(0)
    for side in range(2):
        value_all[side, :, :, HEAD_SIZE:] = jnp.ones((4, length, HEAD_SIZE), jnp.bfloat16)

    @pl.when(jnp.logical_not(has_before))
    def _():
        for group in range(groups):
            kv[FOUR, group] = jnp.zeros(kv.shape[2:], jnp.bfloat16)

    @pl.when(span < 8)
    def _():
        for group in range(groups):
            kv[EIGHT, group] = jnp.zeros(kv.shape[2:], jnp.bfloat16)

    for which in range(2):
        kv_local(0, which).wait()

    def start_chain(slot, step, bit, value):
        @pl.when(bit == value)
        def _():
            chain(0, slot, step).start()

    start_four(0, 0)
    start_chain(TWO, 0, odd_pair, 0)
    start_chain(ONE, 0, odd, 0)
    wait_kv(0)
    start_four(0, 1)
    start_chain(TWO, 1, odd_pair, 0)
    start_chain(ONE, 1, odd, 0)
    query_swap(0).start()
    for step in range(2):
        wait_four(0, step)
        start_eight(0, step)
        start_chain(TWO, step, odd_pair, 1)
    start_kv(1)
    for step in range(2):
        chain(0, TWO, step).wait_recv()
        start_chain(ONE, step, odd, 1)
    for group in range(1, groups):
        for which in range(2):
            kv_local(group, which).wait()
    for group in range(groups):
        query_local(group).wait()
    query_swap(0).wait_recv()
    start_kv(2)
    start_four(1, 0)
    for step in range(2):
        chain(0, ONE, step).wait_recv()
    wait_eight(0)
    wait_kv(1)
    start_four(1, 1)
    prepare(0)
    query_swap(1).start()
    first = top_of([score_block(0, 0, block) for block in range(4)])
    first = stage(0, 1, 0, 0, first)

    def one_head(head, top):
        group = head // sharing
        turn = head % sharing

        @pl.when(turn == 0)
        def _():
            query_swap(group).wait_recv()
            for step in range(2):
                chain(group, ONE, step).wait_recv()
            wait_eight(group)
            prepare(group)

        @pl.when(jnp.logical_and(turn == 1, group + 3 < groups))
        def _():
            start_kv(group + 3)

        @pl.when(jnp.logical_and(turn == sharing - 1, group + 2 < groups))
        def _():
            query_swap(group + 2).start()

        @pl.when(jnp.logical_and(turn == 1, group + 1 < groups))
        def _():
            for step in range(2):
                wait_four(group + 1, step)
                start_eight(group + 1, step)
                chain(group + 1, TWO, step).start()

        @pl.when(jnp.logical_and(turn == sharing - 2, group + 2 < groups))
        def _():
            start_four(group + 2, 0)
            wait_kv(group + 2)
            start_four(group + 2, 1)

        @pl.when(jnp.logical_and(turn == sharing - 1, group + 1 < groups))
        def _():
            for step in range(2):
                chain(group + 1, TWO, step).wait_recv()
                chain(group + 1, ONE, step).start()

        top = stage(head, 0, head - 1, 1, top)
        top = stage(head, 1, head, 0, top)
        out_local(head - 1).start()
        out_swap(head - 1).start()
        return top

    last = lax.fori_loop(1, heads, one_head, first)
    store(
        heads - 1, 1, reduce(jnp.add, [weigh_block(heads - 1, 1, block, last) for block in range(4)])
    )
    out_local(heads - 1).start()
    out_swap(heads - 1).start()

    def settle_group(group, carry):
        for which in range(2):
            kv_swap(group, which).wait_send()
        query_swap(group).wait_send()

        @pl.when(has_after)
        def _():
            four(group, 0).wait_send()
            four(group, 1).wait_send()

        for step in range(2):
            @pl.when(jnp.logical_and(has_before, has_after))
            def _():
                chain(group, EIGHT, step).wait_send()

            chain(group, TWO, step).wait_send()
            chain(group, ONE, step).wait_send()
        return carry

    def settle_head(head, carry):
        out_local(head).wait()
        out_swap(head).wait_send()
        out_swap(head).wait_recv()
        return carry

    lax.fori_loop(0, groups, settle_group, 0)
    lax.fori_loop(0, heads, settle_head, 0)


def fused_attention(sources, query_input, encoded_keys, input_values, spans):
    rows, width = query_input.shape
    groups = encoded_keys.shape[1] // HEAD_SIZE // 2
    heads = width // HEAD_SIZE // 2
    length = 2 * rows
    kept = pl.BlockSpec(memory_space=pl.ANY)
    flops = 4 * 4 * length * length * width // 2
    dma = pltpu.SemaphoreType.DMA
    halves = pl.pallas_call(
        partial(fused_kernel, spans),
        out_shape=jax.ShapeDtypeStruct((2, rows, width // 2), jnp.bfloat16),
        in_specs=[pl.BlockSpec(memory_space=pltpu.SMEM), kept, kept, kept],
        out_specs=kept,
        scratch_shapes=[
            pltpu.VMEM((5, groups, 2, length, HEAD_SIZE), jnp.bfloat16),
            pltpu.VMEM((2, rows, heads * HEAD_SIZE), jnp.bfloat16),
            pltpu.VMEM((2, rows, heads * HEAD_SIZE), jnp.bfloat16),
            pltpu.VMEM((2, 2, length, HEAD_SIZE), jnp.bfloat16),
            pltpu.VMEM((2, 4, length, 2 * HEAD_SIZE), jnp.bfloat16),
            pltpu.VMEM((2, 4, rows, length), jnp.float32),
            dma((groups,)), dma((groups, 2)),
            dma((groups,)), dma((groups,)),
            dma((groups, 2)), dma((groups, 2)),
            dma((groups, 2)), dma((groups, 2)),
            dma((groups, 6)), dma((groups, 6)),
            dma((heads,)), dma((heads,)), dma((heads,)),
        ],
        cost_estimate=pl.CostEstimate(
            flops=flops, bytes_accessed=4 * rows * width, transcendentals=flops // 512
        ),
        compiler_params=pltpu.CompilerParams(
            collective_id=0, has_side_effects=True, vmem_limit_bytes=58 * 1024 * 1024
        ),
    )(sources, query_input, encoded_keys, input_values)
    return jnp.transpose(halves, (1, 0, 2)).reshape(rows, width)


def per_device(query_input, encoded_keys, input_values, sources):
    head_devices = lax.axis_size("head")
    span_count = lax.axis_size("seq")
    if head_devices == 2 and span_count == 16:
        return fused_attention(sources, query_input, encoded_keys, input_values, span_count)
    own_index = lax.axis_index("seq")
    key_heads = encoded_keys.shape[1] // HEAD_SIZE // head_devices
    sharing = query_input.shape[1] // encoded_keys.shape[1]
    distances = [2**power for power in range(1, 31) if 2**power < span_count]
    row = sources[0]
    distance_table = jnp.array(distances, jnp.int32)
    slots = [
        jnp.sum((distance_table < own_index - row[column]).astype(jnp.int32)) for column in (1, 2)
    ]
    choice = jnp.stack(
        [(row[column] >= 0).astype(jnp.int32) for column in range(3)]
        + [jnp.clip(slot, 0, len(distances) - 1) for slot in slots]
    )
    size = min(KEY_HEADS_PER_GROUP, key_heads)
    width = size * HEAD_SIZE
    pieces = [[] for _ in range(head_devices)]
    for number in range(key_heads // size):
        own = gather_heads([encoded_keys, input_values], number, [width, width])
        query = gather_heads([query_input], number, [width * sharing])
        far = {4: passed_along(own, "seq", 4)}
        far[2] = swapped(jnp.where(own_index // 2 % 2 == 0, own, far[4]), "seq", 2)
        far[1] = swapped(jnp.where(own_index % 2 == 0, own, far[2]), "seq", 1)
        for distance in distances[2:]:
            far[distance] = passed_along(far[distance // 2], "seq", distance // 2)
        result = attention(choice, query, [own, far[1]] + [far[d] for d in distances])
        for owner, piece in enumerate(return_tokens(result)):
            pieces[owner].append(piece)
    return jnp.concatenate([piece for owner in pieces for piece in owner], axis=1)


def solution(mesh):
    in_specs = (
        P(("seq", "head"), None),
        P(("seq", "head"), None),
        P(("seq", "head"), None),
        P("seq", None),
    )
    out_specs = P(("seq", "head"), None)
    return jax.shard_map(
        per_device, mesh=mesh, in_specs=in_specs, out_specs=out_specs, check_vma=False
    )
```
